256 devices in a mesh: dp: 2 (over z_hi), seq: 16 (over x, y), fsdp: 8 (over z_lo, core).
Axes of the slice: x: 4, y: 4, z: 8 (z_hi: 2, z_lo: 4; z = z_hi * 4 + z_lo), core: 2. Of those that a mesh axis runs over, the one named last changes fastest.
Arguments:
- video: bfloat16 [16, 32, 128, 3072], P(('dp', 'fsdp'), 'seq'), may hold values from -6 to 6
- norm_gain: float32 [3072], replicated, may hold values from 0.5 to 1.5
- w_query: bfloat16 [3072, 1536], P(None, ('dp', 'fsdp')), may hold values from -0.109375 to 0.109375
- w_key: bfloat16 [3072, 1536], P(None, ('dp', 'fsdp')), may hold values from -0.109375 to 0.109375
- w_value: bfloat16 [3072, 1536], P(None, ('dp', 'fsdp')), may hold values from -0.109375 to 0.109375
- query_gain: float32 [128], replicated, may hold values from 0.1 to 1.9
- key_gain: float32 [128], replicated, may hold values from 0.1 to 1.9
Outputs:
- attended: bfloat16 [16, 32, 128, 1536], P(('dp', 'fsdp'), 'seq')
The draws below stay inside these ranges and needn't reach their ends.
All inputs are finite; a program needn't handle non-finite values.
Results may differ from the reference program's by a relative error of at most 0.0089.
Values may be sent and summed in bfloat16 or wider, within the bound.
No kernel may reach another device: no remote copies, remote signals or barrier semaphores. Data moves between devices by JAX's collectives and lax.ppermute only.
A program may use at most 128 MiB of HBM per device.

```python
import jax
import jax.numpy as jnp
from jax import lax

D = 3072
HEAD_DIM = 128
HD = 1536
FRAMES = 32
PATCHES = 128
VIDEOS = 16


def block_scale(key, dims, shards, smallest, top_value):
    level, own = 1.0, jax.random.fold_in(key, 6)
    for position, blocks in shards:
        draws = jnp.exp(jax.random.uniform(jax.random.fold_in(own, position), (blocks,), jnp.float32, smallest / len(shards), top_value / len(shards)))
        level = level * jnp.repeat(draws, dims[position] // blocks).reshape([-1 if axis == position else 1 for axis in range(len(dims))])
    return level


def noise(own_key, dims, scale, most, cuts=(), held_as=jnp.bfloat16):
    loudness = block_scale(own_key, dims, cuts, -0.22, 0.18) if cuts else 1.0
    result = jax.random.normal(own_key, dims, jnp.float32) * scale * loudness
    return jnp.minimum(jnp.maximum(result, -most), most).astype(held_as)


def setup_inputs(seed: int = 0) -> dict:
    key_list = jax.random.split(jax.random.key(seed), 8)
    return {
        "video": noise(key_list[0], (VIDEOS, FRAMES, PATCHES, D), 1.0, 6.0, ((0, 16), (1, 16))),
        "norm_gain": jnp.clip(1.0 + 0.1 * jax.random.normal(key_list[1], (D,), jnp.float32), 0.5, 1.5),
        "w_query": noise(key_list[2], (D, HD), D ** -0.5, 0.109375, ((1, 16),)),
        "w_key": noise(key_list[3], (D, HD), D ** -0.5, 0.109375, ((1, 16),)),
        "w_value": noise(key_list[4], (D, HD), D ** -0.5, 0.109375, ((1, 16),)),
        "query_gain": jnp.clip(1.0 + 0.18 * jax.random.normal(key_list[5], (HEAD_DIM,), jnp.float32), 0.1, 1.9),
        "key_gain": jnp.clip(1.0 + 0.18 * jax.random.normal(key_list[6], (HEAD_DIM,), jnp.float32), 0.1, 1.9),
    }


def layer_normed(tokens, gain):
    values = tokens.astype(jnp.float32)
    average = lax.optimization_barrier(jnp.mean(values, axis=-1, keepdims=True))
    centred = values - average
    spread = lax.optimization_barrier(jnp.mean(centred * centred, axis=-1, keepdims=True))
    return (centred / jnp.sqrt(spread + 1e-06) * gain).astype(jnp.bfloat16)

def head_normed(rows, gain, head_dim):
    shaped = rows.astype(jnp.float32).reshape(rows.shape[:-1] + (rows.shape[-1] // head_dim, head_dim))
    square = lax.optimization_barrier(jnp.mean(shaped * shaped, axis=-1, keepdims=True))
    return shaped / jnp.sqrt(square + 1e-06) * gain

def attend(query_rows, key_rows, value_rows, query_gain, key_gain):
    head_dim = query_gain.shape[0]
    query_unit = head_normed(query_rows, query_gain, head_dim)
    key_unit = head_normed(key_rows, key_gain, head_dim)
    values_split = value_rows.astype(jnp.float32).reshape(query_unit.shape)
    scores = jnp.einsum('fphd,gphd->phfg', query_unit, key_unit, precision=lax.Precision.HIGHEST) / jnp.sqrt(jnp.float32(head_dim))
    weights = jnp.exp(scores)
    probs = (weights / lax.optimization_barrier(jnp.sum(weights, axis=-1, keepdims=True))).astype(jnp.bfloat16)
    output = jnp.einsum('phfg,gphd->fphd', probs.astype(jnp.float32), values_split, precision=lax.Precision.HIGHEST)
    return output.reshape(query_rows.shape).astype(jnp.bfloat16)

def reference(video, norm_gain, w_query, w_key, w_value, query_gain, key_gain):

    def per_video(frames):
        normed = layer_normed(frames, norm_gain)
        flat = normed.reshape(-1, frames.shape[-1])
        shape_out = frames.shape[:-1] + (w_query.shape[1],)
        query_rows = jnp.dot(flat, w_query, preferred_element_type=jnp.float32).astype(jnp.bfloat16).reshape(shape_out)
        key_rows = jnp.dot(flat, w_key, preferred_element_type=jnp.float32).astype(jnp.bfloat16).reshape(shape_out)
        value_rows = jnp.dot(flat, w_value, preferred_element_type=jnp.float32).astype(jnp.bfloat16).reshape(shape_out)
        return attend(query_rows, key_rows, value_rows, query_gain, key_gain)
    return lax.map(per_video, video)
```

```python
import jax
import jax.numpy as jnp
from jax import lax
from jax.experimental import pallas as pl
from jax.experimental.pallas import tpu as pltpu
from jax.sharding import PartitionSpec as P

AXES = ("dp", "seq", "fsdp")
SHIFTS = (0, 1, 3, 2)


def place(x, y, z, core):
    return ((z // 4) * 16 + x * 4 + y) * 8 + (z % 4) * 2 + core


def every_place():
    return [(x, y, z, c) for x in range(4) for y in range(4) for z in range(8) for c in range(2)]


def scatter_perm(shift):
    pairs = []
    for x in range(4):
        for y in range(4):
            j = (x + y) % 4
            for a in range(2):
                for c in range(2):
                    z = 2 * j + a
                    pairs.append((place(x, y, z, c), place(x, y, (z + 2 * shift) % 8, c)))
    return pairs


def line_perm(shift):
    pairs = []
    for x, y, z, c in every_place():
        to = ((x + shift) % 4, y) if c == 0 else (x, (y + shift) % 4)
        pairs.append((place(x, y, z, c), place(to[0], to[1], z, c)))
    return pairs


def norm_kernel(video_ref, gain_ref, out_ref):
    values = video_ref[0].astype(jnp.float32)
    average = jnp.mean(values, axis=-1, keepdims=True)
    centred = values - average
    spread = jnp.mean(centred * centred, axis=-1, keepdims=True)
    normed = centred * lax.rsqrt(spread + 1e-06) * gain_ref[...][None]
    for s in range(out_ref.shape[0]):
        part = [normed[f, 8 * s : 8 * s + 8] for f in range(2)]
        out_ref[s] = jnp.concatenate(part, axis=0).astype(jnp.bfloat16)


def layer_normed(video, gain):
    d = video.shape[-1]
    steps = 4
    return pl.pallas_call(
        norm_kernel,
        grid=(steps,),
        in_specs=[
            pl.BlockSpec((1, 2, 128 // steps, d), lambda i: (0, 0, i, 0)),
            pl.BlockSpec((1, d), lambda i: (0, 0)),
        ],
        out_specs=pl.BlockSpec((16 // steps, 16, d), lambda i: (i, 0, 0)),
        out_shape=jax.ShapeDtypeStruct((16, 16, d), jnp.bfloat16),
        compiler_params=pltpu.CompilerParams(vmem_limit_bytes=40 * 2**20),
        name="norm_rows",
    )(video, gain.reshape(1, d))


NT = (((1,), (1,)), ((), ()))


def attend_kernel(group_ref, r0, r1, r2, r3, w_ref, qg_ref, kg_ref, out_ref, rows, weights, acc):
    t = pl.program_id(0)
    for i, ref in enumerate((r0, r1, r2, r3)):
        rows[256 * i : 256 * i + 256, :] = ref[...]
    for m in range(3):
        for blk in range(4):
            at = 384 * m + 96 * blk
            weights[at : at + 96, :] = w_ref[0, blk, 96 * m : 96 * m + 96, :]
    product = lax.dot_general(rows[...], weights[...], NT, preferred_element_type=jnp.float32)

    @pl.when(t == 0)
    def _():
        acc[...] = product

    @pl.when(t > 0)
    def _():
        acc[...] += product

    @pl.when(t == pl.num_programs(0) - 1)
    def _():
        gains = qg_ref[...] * kg_ref[...] * (128.0**-0.5)
        row_patch = lax.broadcasted_iota(jnp.int32, (256, 256), 0) % 8
        col_patch = lax.broadcasted_iota(jnp.int32, (256, 256), 1) % 8
        same = row_patch == col_patch
        for i in range(4):
            for h in range(3):
                part = acc[256 * i : 256 * i + 256, :]
                q_rows = part[:, 128 * h : 128 * h + 128].astype(jnp.bfloat16)
                k = part[:, 384 + 128 * h : 512 + 128 * h].astype(jnp.bfloat16).astype(jnp.float32)
                v = part[:, 768 + 128 * h : 896 + 128 * h].astype(jnp.bfloat16)
                q = q_rows.astype(jnp.float32)
                q_scale = lax.rsqrt(jnp.mean(q * q, axis=-1, keepdims=True) + 1e-06)
                k_scale = lax.rsqrt(jnp.mean(k * k, axis=-1, keepdims=True) + 1e-06)
                k_unit = (k * k_scale * gains).astype(jnp.bfloat16)
                scores = lax.dot_general(q_rows, k_unit, NT, preferred_element_type=jnp.float32)
                exps = jnp.where(same, jnp.exp(scores * q_scale), 0.0)
                probs = (exps / jnp.sum(exps, axis=-1, keepdims=True)).astype(jnp.bfloat16)
                out = jnp.dot(probs, v, preferred_element_type=jnp.float32).astype(jnp.bfloat16)
                out_ref[:, 16 * i : 16 * i + 16, 128 * h : 128 * h + 128] = out.reshape(16, 16, 128)


def attend(pieces, gathered, group, query_gain, key_gain):
    d = pieces[0].shape[-1]
    quarter = d // 4
    spec = pl.BlockSpec((256, quarter), lambda t, g: (0, (t - g[0] + 4) % 4))
    gain_spec = pl.BlockSpec((1, 128), lambda t, g: (0, 0))
    return pl.pallas_call(
        attend_kernel,
        grid_spec=pltpu.PrefetchScalarGridSpec(
            num_scalar_prefetch=1,
            grid=(4,),
            in_specs=[spec] * 4
            + [pl.BlockSpec((1, 4, 288, quarter), lambda t, g: (t, 0, 0, 0)), gain_spec, gain_spec],
            out_specs=pl.BlockSpec((16, 64, 384), lambda t, g: (0, 0, 0)),
            scratch_shapes=[
                pltpu.VMEM((1024, quarter), jnp.bfloat16),
                pltpu.VMEM((1152, quarter), jnp.bfloat16),
                pltpu.VMEM((1024, 1152), jnp.float32),
            ],
        ),
        out_shape=jax.ShapeDtypeStruct((16, 64, 384), jnp.bfloat16),
        compiler_params=pltpu.CompilerParams(vmem_limit_bytes=50 * 2**20),
        name="project_attend",
    )(group, *pieces, gathered, query_gain.reshape(1, 128), key_gain.reshape(1, 128))


def sources(core):
    found = {}
    for x in range(4):
        for y in range(4):
            for piece, shift in enumerate(SHIFTS):
                s = ((x - shift) % 4) * 4 + y if core == 0 else x * 4 + (y - shift) % 4
                found[s, (x + y) % 4] = (4 * x + y, piece)
    return found


def assemble_kernel(core_ref, recv_ref, out_ref):
    for core in range(2):

        @pl.when(core_ref[0] == core)
        def _(found=sources(core)):
            for s in range(0, 16, 2):
                for j in range(4):
                    src, piece = found[s, j]
                    low = recv_ref[src, 16 * piece : 16 * piece + 16, :].astype(jnp.float32)
                    src, piece = found[s + 1, j]
                    high = recv_ref[src, 16 * piece : 16 * piece + 16, :].astype(jnp.float32)
                    for f in range(2):
                        both = jnp.concatenate([low[8 * f : 8 * f + 8], high[8 * f : 8 * f + 8]], axis=0)
                        out_ref[0, f, 8 * s : 8 * s + 16, 384 * j : 384 * j + 384] = both.astype(jnp.bfloat16)


def assemble(received, core):
    return pl.pallas_call(
        assemble_kernel,
        in_specs=[pl.BlockSpec(memory_space=pltpu.SMEM), pl.BlockSpec(memory_space=pltpu.VMEM)],
        out_specs=pl.BlockSpec(memory_space=pltpu.VMEM),
        out_shape=jax.ShapeDtypeStruct((1, 2, 128, 1536), jnp.bfloat16),
        compiler_params=pltpu.CompilerParams(vmem_limit_bytes=40 * 2**20),
        name="assemble_heads",
    )(core, received)


def shards(video, norm_gain, w_query, w_key, w_value, query_gain, key_gain):
    seq = lax.axis_index("seq")
    fsdp = lax.axis_index("fsdp")
    pair = lax.axis_index("dp") * 2 + fsdp // 4
    core = (fsdp % 2).astype(jnp.int32).reshape(1)
    group = (seq // 4 + seq % 4) % 4
    d = video.shape[-1]
    quarter = d // 4

    columns = [w.T for w in (w_query, w_key, w_value)]
    quarters = [
        jnp.concatenate([c[:, quarter * r : quarter * (r + 1)] for c in columns], axis=0) for r in range(4)
    ]
    with jax.named_scope("scatter"):
        mine = [quarters[0]] + [lax.ppermute(quarters[r], AXES, scatter_perm(r)) for r in (1, 3, 2)]
    part = lax.select_n((pair - group + 4) % 4, mine[0], mine[1], mine[3], mine[2])
    gathered = lax.all_gather(part, ("dp", "fsdp"), axis=0, tiled=True)
    gathered = gathered.reshape(4, 4, 288, quarter)

    normed = layer_normed(video, norm_gain)
    with jax.named_scope("rows_home"):
        home = lax.all_to_all(normed, "seq", split_axis=0, concat_axis=0, tiled=True).reshape(256, d)
    with jax.named_scope("rows_line"):
        pieces = [home] + [lax.ppermute(home, AXES, line_perm(s)) for s in SHIFTS[1:]]
    output = attend(pieces, gathered, group.astype(jnp.int32).reshape(1), query_gain, key_gain)
    with jax.named_scope("heads_back"):
        received = lax.all_to_all(output, "seq", split_axis=0, concat_axis=0, tiled=True)
    return assemble(received, core)


def solution(mesh):
    in_specs = (
        P(("dp", "fsdp"), "seq", None, None),
        P(),
        P(None, ("dp", "fsdp")),
        P(None, ("dp", "fsdp")),
        P(None, ("dp", "fsdp")),
        P(),
        P(),
    )
    out_specs = P(("dp", "fsdp"), "seq", None, None)
    return jax.shard_map(shards, mesh=mesh, in_specs=in_specs, out_specs=out_specs, check_vma=False)
```

```python
import jax
import jax.numpy as jnp
from jax import lax
from jax.experimental import pallas as pl
from jax.experimental.pallas import tpu as pltpu
from jax.sharding import PartitionSpec as P

AXES = ("dp", "seq", "fsdp")
SHIFTS = (0, 1, 3, 2)


def place(x, y, z, core):
    return ((z // 4) * 16 + x * 4 + y) * 8 + (z % 4) * 2 + core


def every_place():
    return [(x, y, z, c) for x in range(4) for y in range(4) for z in range(8) for c in range(2)]


def scatter_perm(shift):
    pairs = []
    for x in range(4):
        for y in range(4):
            j = (x + y) % 4
            for a in range(2):
                for c in range(2):
                    z = 2 * j + a
                    pairs.append((place(x, y, z, c), place(x, y, (z + 2 * shift) % 8, c)))
    return pairs


def line_perm(shift):
    pairs = []
    for x, y, z, c in every_place():
        to = ((x + shift) % 4, y) if c == 0 else (x, (y + shift) % 4)
        pairs.append((place(x, y, z, c), place(to[0], to[1], z, c)))
    return pairs


def norm_kernel(video_ref, gain_ref, out_ref):
    values = video_ref[0].astype(jnp.float32)
    average = jnp.mean(values, axis=-1, keepdims=True)
    centred = values - average
    spread = jnp.mean(centred * centred, axis=-1, keepdims=True)
    normed = centred * lax.rsqrt(spread + 1e-06) * gain_ref[...][None]
    for s in range(out_ref.shape[0]):
        part = [normed[f, 8 * s : 8 * s + 8] for f in range(2)]
        out_ref[s] = jnp.concatenate(part, axis=0).astype(jnp.bfloat16)


def layer_normed(video, gain):
    d = video.shape[-1]
    steps = 4
    return pl.pallas_call(
        norm_kernel,
        grid=(steps,),
        in_specs=[
            pl.BlockSpec((1, 2, 128 // steps, d), lambda i: (0, 0, i, 0)),
            pl.BlockSpec((1, d), lambda i: (0, 0)),
        ],
        out_specs=pl.BlockSpec((16 // steps, 16, d), lambda i: (i, 0, 0)),
        out_shape=jax.ShapeDtypeStruct((16, 16, d), jnp.bfloat16),
        compiler_params=pltpu.CompilerParams(vmem_limit_bytes=40 * 2**20),
        name="norm_rows",
    )(video, gain.reshape(1, d))


NT = (((1,), (1,)), ((), ()))


def attend_kernel(group_ref, r0, r1, r2, r3, w_ref, qg_ref, kg_ref, out_ref, rows, weights, acc):
    t = pl.program_id(0)
    for i, ref in enumerate((r0, r1, r2, r3)):
        rows[256 * i : 256 * i + 256, :] = ref[...]
    for m in range(3):
        for blk in range(4):
            at = 384 * m + 96 * blk
            weights[at : at + 96, :] = w_ref[0, blk, 96 * m : 96 * m + 96, :]
    product = lax.dot_general(rows[...], weights[...], NT, preferred_element_type=jnp.float32)

    @pl.when(t == 0)
    def _():
        acc[...] = product

    @pl.when(t > 0)
    def _():
        acc[...] += product

    @pl.when(t == pl.num_programs(0) - 1)
    def _():
        gains = qg_ref[...] * kg_ref[...] * (128.0**-0.5)
        row_patch = lax.broadcasted_iota(jnp.int32, (256, 256), 0) % 8
        col_patch = lax.broadcasted_iota(jnp.int32, (256, 256), 1) % 8
        same = row_patch == col_patch
        for i in range(4):
            for h in range(3):
                part = acc[256 * i : 256 * i + 256, :]
                q_rows = part[:, 128 * h : 128 * h + 128].astype(jnp.bfloat16)
                k = part[:, 384 + 128 * h : 512 + 128 * h].astype(jnp.bfloat16).astype(jnp.float32)
                v = part[:, 768 + 128 * h : 896 + 128 * h].astype(jnp.bfloat16)
                q = q_rows.astype(jnp.float32)
                q_scale = lax.rsqrt(jnp.mean(q * q, axis=-1, keepdims=True) + 1e-06)
                k_scale = lax.rsqrt(jnp.mean(k * k, axis=-1, keepdims=True) + 1e-06)
                k_unit = (k * k_scale * gains).astype(jnp.bfloat16)
                scores = lax.dot_general(q_rows, k_unit, NT, preferred_element_type=jnp.float32)
                exps = jnp.where(same, jnp.exp(scores * q_scale), 0.0)
                probs = (exps / jnp.sum(exps, axis=-1, keepdims=True)).astype(jnp.bfloat16)
                out = jnp.dot(probs, v, preferred_element_type=jnp.float32).astype(jnp.bfloat16)
                out_ref[:, 16 * i : 16 * i + 16, 128 * h : 128 * h + 128] = out.reshape(16, 16, 128)


def attend(pieces, gathered, group, query_gain, key_gain):
    d = pieces[0].shape[-1]
    quarter = d // 4
    spec = pl.BlockSpec((256, quarter), lambda t, g: (0, (t - g[0] + 4) % 4))
    gain_spec = pl.BlockSpec((1, 128), lambda t, g: (0, 0))
    return pl.pallas_call(
        attend_kernel,
        grid_spec=pltpu.PrefetchScalarGridSpec(
            num_scalar_prefetch=1,
            grid=(4,),
            in_specs=[spec] * 4
            + [pl.BlockSpec((1, 4, 288, quarter), lambda t, g: (t, 0, 0, 0)), gain_spec, gain_spec],
            out_specs=pl.BlockSpec((16, 64, 384), lambda t, g: (0, 0, 0)),
            scratch_shapes=[
                pltpu.VMEM((1024, quarter), jnp.bfloat16),
                pltpu.VMEM((1152, quarter), jnp.bfloat16),
                pltpu.VMEM((1024, 1152), jnp.float32),
            ],
        ),
        out_shape=jax.ShapeDtypeStruct((16, 64, 384), jnp.bfloat16),
        compiler_params=pltpu.CompilerParams(vmem_limit_bytes=50 * 2**20),
        name="project_attend",
    )(group, *pieces, gathered, query_gain.reshape(1, 128), key_gain.reshape(1, 128))


def sources(core):
    found = {}
    for x in range(4):
        for y in range(4):
            for piece, shift in enumerate(SHIFTS):
                s = ((x - shift) % 4) * 4 + y if core == 0 else x * 4 + (y - shift) % 4
                found[s, (x + y) % 4] = (4 * x + y, piece)
    return found


def assemble_kernel(core_ref, recv_ref, out_ref):
    for core in range(2):

        @pl.when(core_ref[0] == core)
        def _(found=sources(core)):
            for s in range(0, 16, 2):
                for j in range(4):
                    src, piece = found[s, j]
                    low = recv_ref[src, 16 * piece : 16 * piece + 16, :].astype(jnp.float32)
                    src, piece = found[s + 1, j]
                    high = recv_ref[src, 16 * piece : 16 * piece + 16, :].astype(jnp.float32)
                    for f in range(2):
                        both = jnp.concatenate([low[8 * f : 8 * f + 8], high[8 * f : 8 * f + 8]], axis=0)
                        out_ref[0, f, 8 * s : 8 * s + 16, 384 * j : 384 * j + 384] = both.astype(jnp.bfloat16)


def assemble(received, core):
    return pl.pallas_call(
        assemble_kernel,
        in_specs=[pl.BlockSpec(memory_space=pltpu.SMEM), pl.BlockSpec(memory_space=pltpu.VMEM)],
        out_specs=pl.BlockSpec(memory_space=pltpu.VMEM),
        out_shape=jax.ShapeDtypeStruct((1, 2, 128, 1536), jnp.bfloat16),
        compiler_params=pltpu.CompilerParams(vmem_limit_bytes=40 * 2**20),
        name="assemble_heads",
    )(core, received)


def shards(video, norm_gain, w_query, w_key, w_value, query_gain, key_gain):
    seq = lax.axis_index("seq")
    fsdp = lax.axis_index("fsdp")
    pair = lax.axis_index("dp") * 2 + fsdp // 4
    core = (fsdp % 2).astype(jnp.int32).reshape(1)
    group = (seq // 4 + seq % 4) % 4
    d = video.shape[-1]
    quarter = d // 4

    columns = [w.T for w in (w_query, w_key, w_value)]
    quarters = [
        jnp.concatenate([c[:, quarter * r : quarter * (r + 1)] for c in columns], axis=0) for r in range(4)
    ]
    with jax.named_scope("scatter"):
        mine = [quarters[0]] + [lax.ppermute(quarters[r], AXES, scatter_perm(r)) for r in (1, 3, 2)]
    normed = layer_normed(video, norm_gain)
    with jax.named_scope("rows_home"):
        home = lax.all_to_all(normed, "seq", split_axis=0, concat_axis=0, tiled=True).reshape(256, d)
    mine, home = lax.optimization_barrier((mine, home))
    part = lax.select_n((pair - group + 4) % 4, mine[0], mine[1], mine[3], mine[2])
    gathered = lax.all_gather(part, ("dp", "fsdp"), axis=0, tiled=True)
    gathered = gathered.reshape(4, 4, 288, quarter)

    with jax.named_scope("rows_line"):
        pieces = [home] + [lax.ppermute(home, AXES, line_perm(s)) for s in SHIFTS[1:]]
    output = attend(pieces, gathered, group.astype(jnp.int32).reshape(1), query_gain, key_gain)
    with jax.named_scope("heads_back"):
        received = lax.all_to_all(output, "seq", split_axis=0, concat_axis=0, tiled=True)
    return assemble(received, core)


def solution(mesh):
    in_specs = (
        P(("dp", "fsdp"), "seq", None, None),
        P(),
        P(None, ("dp", "fsdp")),
        P(None, ("dp", "fsdp")),
        P(None, ("dp", "fsdp")),
        P(),
        P(),
    )
    out_specs = P(("dp", "fsdp"), "seq", None, None)
    return jax.shard_map(shards, mesh=mesh, in_specs=in_specs, out_specs=out_specs, check_vma=False)
```

```python
import jax
import jax.numpy as jnp
from jax import lax
from jax.experimental import pallas as pl
from jax.experimental.pallas import tpu as pltpu
from jax.sharding import PartitionSpec as P

AXES = ("dp", "seq", "fsdp")
SHIFTS = (0, 1, 3, 2)


def place(x, y, z, core):
    return ((z // 4) * 16 + x * 4 + y) * 8 + (z % 4) * 2 + core


def every_place():
    return [(x, y, z, c) for x in range(4) for y in range(4) for z in range(8) for c in range(2)]


def scatter_perm(shift):
    pairs = []
    for x in range(4):
        for y in range(4):
            j = (x + y) % 4
            origin = (x + 2) % 4 if shift == 2 else x
            for a in range(2):
                for c in range(2):
                    z = 2 * j + a
                    pairs.append((place(origin, y, z, c), place(x, y, (z + 2 * shift) % 8, c)))
    return pairs


def line_perm(shift):
    pairs = []
    for x, y, z, c in every_place():
        to = ((x + shift) % 4, y) if c == 0 else (x, (y + shift) % 4)
        pairs.append((place(x, y, z, c), place(to[0], to[1], z, c)))
    return pairs


def norm_kernel(video_ref, gain_ref, out_ref):
    values = video_ref[0].astype(jnp.float32)
    average = jnp.mean(values, axis=-1, keepdims=True)
    centred = values - average
    spread = jnp.mean(centred * centred, axis=-1, keepdims=True)
    normed = centred * lax.rsqrt(spread + 1e-06) * gain_ref[...][None]
    for s in range(out_ref.shape[0]):
        part = [normed[f, 8 * s : 8 * s + 8] for f in range(2)]
        out_ref[s] = jnp.concatenate(part, axis=0).astype(jnp.bfloat16)


def layer_normed(video, gain):
    d = video.shape[-1]
    steps = 4
    return pl.pallas_call(
        norm_kernel,
        grid=(steps,),
        in_specs=[
            pl.BlockSpec((1, 2, 128 // steps, d), lambda i: (0, 0, i, 0)),
            pl.BlockSpec((1, d), lambda i: (0, 0)),
        ],
        out_specs=pl.BlockSpec((16 // steps, 16, d), lambda i: (i, 0, 0)),
        out_shape=jax.ShapeDtypeStruct((16, 16, d), jnp.bfloat16),
        compiler_params=pltpu.CompilerParams(vmem_limit_bytes=40 * 2**20),
        name="norm_rows",
    )(video, gain.reshape(1, d))


NT = (((1,), (1,)), ((), ()))


def attend_kernel(group_ref, r0, r1, r2, r3, w_ref, qg_ref, kg_ref, out_ref, rows, weights, acc):
    t = pl.program_id(0)
    for i, ref in enumerate((r0, r1, r2, r3)):
        rows[256 * i : 256 * i + 256, :] = ref[...]
    for m in range(3):
        for blk in range(4):
            at = 384 * m + 96 * blk
            weights[at : at + 96, :] = w_ref[0, blk, 96 * m : 96 * m + 96, :]
    product = lax.dot_general(rows[...], weights[...], NT, preferred_element_type=jnp.float32)

    @pl.when(t == 0)
    def _():
        acc[...] = product

    @pl.when(t > 0)
    def _():
        acc[...] += product

    @pl.when(t == pl.num_programs(0) - 1)
    def _():
        gains = qg_ref[...] * kg_ref[...] * (128.0**-0.5)
        row_patch = lax.broadcasted_iota(jnp.int32, (256, 256), 0) % 8
        col_patch = lax.broadcasted_iota(jnp.int32, (256, 256), 1) % 8
        same = row_patch == col_patch
        for i in range(4):
            for h in range(3):
                part = acc[256 * i : 256 * i + 256, :]
                q_rows = part[:, 128 * h : 128 * h + 128].astype(jnp.bfloat16)
                k = part[:, 384 + 128 * h : 512 + 128 * h].astype(jnp.bfloat16).astype(jnp.float32)
                v = part[:, 768 + 128 * h : 896 + 128 * h].astype(jnp.bfloat16)
                q = q_rows.astype(jnp.float32)
                q_scale = lax.rsqrt(jnp.mean(q * q, axis=-1, keepdims=True) + 1e-06)
                k_scale = lax.rsqrt(jnp.mean(k * k, axis=-1, keepdims=True) + 1e-06)
                k_unit = (k * k_scale * gains).astype(jnp.bfloat16)
                scores = lax.dot_general(q_rows, k_unit, NT, preferred_element_type=jnp.float32)
                exps = jnp.where(same, jnp.exp(scores * q_scale), 0.0)
                probs = (exps / jnp.sum(exps, axis=-1, keepdims=True)).astype(jnp.bfloat16)
                out = jnp.dot(probs, v, preferred_element_type=jnp.float32).astype(jnp.bfloat16)
                out_ref[:, 16 * i : 16 * i + 16, 128 * h : 128 * h + 128] = out.reshape(16, 16, 128)


def attend(pieces, gathered, group, query_gain, key_gain):
    d = pieces[0].shape[-1]
    quarter = d // 4
    spec = pl.BlockSpec((256, quarter), lambda t, g: (0, (t - g[0] + 4) % 4))
    gain_spec = pl.BlockSpec((1, 128), lambda t, g: (0, 0))
    return pl.pallas_call(
        attend_kernel,
        grid_spec=pltpu.PrefetchScalarGridSpec(
            num_scalar_prefetch=1,
            grid=(4,),
            in_specs=[spec] * 4
            + [pl.BlockSpec((1, 4, 288, quarter), lambda t, g: (t, 0, 0, 0)), gain_spec, gain_spec],
            out_specs=pl.BlockSpec((16, 64, 384), lambda t, g: (0, 0, 0)),
            scratch_shapes=[
                pltpu.VMEM((1024, quarter), jnp.bfloat16),
                pltpu.VMEM((1152, quarter), jnp.bfloat16),
                pltpu.VMEM((1024, 1152), jnp.float32),
            ],
        ),
        out_shape=jax.ShapeDtypeStruct((16, 64, 384), jnp.bfloat16),
        compiler_params=pltpu.CompilerParams(vmem_limit_bytes=50 * 2**20),
        name="project_attend",
    )(group, *pieces, gathered, query_gain.reshape(1, 128), key_gain.reshape(1, 128))


def sources(core):
    found = {}
    for x in range(4):
        for y in range(4):
            for piece, shift in enumerate(SHIFTS):
                s = ((x - shift) % 4) * 4 + y if core == 0 else x * 4 + (y - shift) % 4
                found[s, (x + y) % 4] = (4 * x + y, piece)
    return found


def assemble_kernel(core_ref, recv_ref, out_ref):
    for core in range(2):

        @pl.when(core_ref[0] == core)
        def _(found=sources(core)):
            for s in range(0, 16, 2):
                for j in range(4):
                    src, piece = found[s, j]
                    low = recv_ref[src, 16 * piece : 16 * piece + 16, :].astype(jnp.float32)
                    src, piece = found[s + 1, j]
                    high = recv_ref[src, 16 * piece : 16 * piece + 16, :].astype(jnp.float32)
                    for f in range(2):
                        both = jnp.concatenate([low[8 * f : 8 * f + 8], high[8 * f : 8 * f + 8]], axis=0)
                        out_ref[0, f, 8 * s : 8 * s + 16, 384 * j : 384 * j + 384] = both.astype(jnp.bfloat16)


def assemble(received, core):
    return pl.pallas_call(
        assemble_kernel,
        in_specs=[pl.BlockSpec(memory_space=pltpu.SMEM), pl.BlockSpec(memory_space=pltpu.VMEM)],
        out_specs=pl.BlockSpec(memory_space=pltpu.VMEM),
        out_shape=jax.ShapeDtypeStruct((1, 2, 128, 1536), jnp.bfloat16),
        compiler_params=pltpu.CompilerParams(vmem_limit_bytes=40 * 2**20),
        name="assemble_heads",
    )(core, received)


def shards(video, norm_gain, w_query, w_key, w_value, query_gain, key_gain):
    seq = lax.axis_index("seq")
    fsdp = lax.axis_index("fsdp")
    pair = lax.axis_index("dp") * 2 + fsdp // 4
    core = (fsdp % 2).astype(jnp.int32).reshape(1)
    group = (seq // 4 + seq % 4) % 4
    d = video.shape[-1]
    quarter = d // 4

    columns = [w.T for w in (w_query, w_key, w_value)]
    quarters = [
        jnp.concatenate([c[:, quarter * r : quarter * (r + 1)] for c in columns], axis=0) for r in range(4)
    ]
    with jax.named_scope("scatter"):
        mine = [quarters[0]] + [lax.ppermute(quarters[r], AXES, scatter_perm(r)) for r in (1, 3, 2)]
    normed = layer_normed(video, norm_gain)
    with jax.named_scope("rows_home"):
        home = lax.all_to_all(normed, "seq", split_axis=0, concat_axis=0, tiled=True).reshape(256, d)
    mine, home = lax.optimization_barrier((mine, home))
    part = lax.select_n((pair - group + 4) % 4, mine[0], mine[1], mine[3], mine[2])
    gathered = lax.all_gather(part, ("dp", "fsdp"), axis=0, tiled=True)
    gathered = gathered.reshape(4, 4, 288, quarter)

    with jax.named_scope("rows_line"):
        pieces = [home] + [lax.ppermute(home, AXES, line_perm(s)) for s in SHIFTS[1:]]
    output = attend(pieces, gathered, group.astype(jnp.int32).reshape(1), query_gain, key_gain)
    with jax.named_scope("heads_back"):
        received = lax.all_to_all(output, "seq", split_axis=0, concat_axis=0, tiled=True)
    return assemble(received, core)


def solution(mesh):
    in_specs = (
        P(("dp", "fsdp"), "seq", None, None),
        P(),
        P(None, ("dp", "fsdp")),
        P(None, ("dp", "fsdp")),
        P(None, ("dp", "fsdp")),
        P(),
        P(),
    )
    out_specs = P(("dp", "fsdp"), "seq", None, None)
    return jax.shard_map(shards, mesh=mesh, in_specs=in_specs, out_specs=out_specs, check_vma=False)
```

```python
import jax
import jax.numpy as jnp
from jax import lax
from jax.experimental import pallas as pl
from jax.experimental.pallas import tpu as pltpu
from jax.sharding import PartitionSpec as P

AXES = ("dp", "seq", "fsdp")
SHIFTS = (0, 1, 3, 2)


def place(x, y, z, core):
    return ((z // 4) * 16 + x * 4 + y) * 8 + (z % 4) * 2 + core


def every_place():
    return [(x, y, z, c) for x in range(4) for y in range(4) for z in range(8) for c in range(2)]


def scatter_perm(shift):
    pairs = []
    for x in range(4):
        for y in range(4):
            j = (x + y) % 4
            origin = (x + 2) % 4 if shift == 2 else x
            for a in range(2):
                for c in range(2):
                    z = 2 * j + a
                    pairs.append((place(origin, y, z, c), place(x, y, (z + 2 * shift) % 8, c)))
    return pairs


def line_perm(shift):
    pairs = []
    for x, y, z, c in every_place():
        to = ((x + shift) % 4, y) if c == 0 else (x, (y + shift) % 4)
        pairs.append((place(x, y, z, c), place(to[0], to[1], z, c)))
    return pairs


def ring_perm(step):
    return [(place(x, y, z, c), place(x, y, (z + step) % 8, c)) for x, y, z, c in every_place()]


def swap_perm():
    return [(place(x, y, z, c), place(x, y, z, 1 - c)) for x, y, z, c in every_place()]


def pack_kernel(wq, wk, wv, q0, q1, q2, q3, columns, packed, sems, out_sems):
    fetches = [pltpu.make_async_copy(w, columns.at[m], sems.at[m]) for m, w in enumerate((wq, wk, wv))]
    for copy in fetches:
        copy.start()
    for copy in fetches:
        copy.wait()
    height, quarter = columns.shape[1], packed.shape[2]
    stores = []
    for r, out in ((1, q1), (2, q2), (3, q3), (0, q0)):
        for m in range(3):
            packed[r, height * m : height * (m + 1), :] = columns[m, :, quarter * r : quarter * (r + 1)]
        store = pltpu.make_async_copy(packed.at[r], out, out_sems.at[r])
        store.start()
        stores.append(store)
    for store in stores:
        store.wait()


def pack(columns):
    height, d = columns[0].shape
    anywhere = pl.BlockSpec(memory_space=pl.ANY)
    return pl.pallas_call(
        pack_kernel,
        in_specs=[anywhere] * 3,
        out_specs=[anywhere] * 4,
        out_shape=[jax.ShapeDtypeStruct((3 * height, d // 4), jnp.bfloat16)] * 4,
        scratch_shapes=[
            pltpu.VMEM((3, height, d), jnp.bfloat16),
            pltpu.VMEM((4, 3 * height, d // 4), jnp.bfloat16),
            pltpu.SemaphoreType.DMA((3,)),
            pltpu.SemaphoreType.DMA((4,)),
        ],
        compiler_params=pltpu.CompilerParams(vmem_limit_bytes=58 * 2**20),
        name="pack_weights",
    )(*columns)


def norm_kernel(video_ref, gain_ref, out_ref):
    values = video_ref[0].astype(jnp.float32)
    average = jnp.mean(values, axis=-1, keepdims=True)
    centred = values - average
    spread = jnp.mean(centred * centred, axis=-1, keepdims=True)
    normed = centred * lax.rsqrt(spread + 1e-06) * gain_ref[...][None]
    for s in range(out_ref.shape[0]):
        part = [normed[f, 8 * s : 8 * s + 8] for f in range(2)]
        out_ref[s] = jnp.concatenate(part, axis=0).astype(jnp.bfloat16)


def layer_normed(video, gain):
    d = video.shape[-1]
    steps = 4
    return pl.pallas_call(
        norm_kernel,
        grid=(steps,),
        in_specs=[
            pl.BlockSpec((1, 2, 128 // steps, d), lambda i: (0, 0, i, 0)),
            pl.BlockSpec((1, d), lambda i: (0, 0)),
        ],
        out_specs=pl.BlockSpec((16 // steps, 16, d), lambda i: (i, 0, 0)),
        out_shape=jax.ShapeDtypeStruct((16, 16, d), jnp.bfloat16),
        compiler_params=pltpu.CompilerParams(vmem_limit_bytes=16 * 2**20),
        name="norm_rows",
    )(video, gain.reshape(1, d))


def choose_kernel(where, q0, q1, q2, q3, out_ref):
    quarter = (where[0] // 2 - where[1] + 4) % 4
    for r, ref in enumerate((q0, q1, q2, q3)):

        @pl.when(quarter == r)
        def _(ref=ref):
            out_ref[...] = ref[...]


def choose(where, parts):
    vmem = pl.BlockSpec(memory_space=pltpu.VMEM)
    return pl.pallas_call(
        choose_kernel,
        in_specs=[pl.BlockSpec(memory_space=pltpu.SMEM)] + [vmem] * 4,
        out_specs=vmem,
        out_shape=jax.ShapeDtypeStruct(parts[0].shape, parts[0].dtype),
        compiler_params=pltpu.CompilerParams(vmem_limit_bytes=8 * 2**20),
        name="choose_quarter",
    )(where, *parts)


def halve_kernel(up, down, up_half, down_half):
    width = up_half.shape[1]
    up_half[...] = up[:, :width]
    down_half[...] = down[:, width:]


def halve(up, down):
    vmem = pl.BlockSpec(memory_space=pltpu.VMEM)
    half = jax.ShapeDtypeStruct((up.shape[0], up.shape[1] // 2), up.dtype)
    return pl.pallas_call(
        halve_kernel,
        in_specs=[vmem] * 2,
        out_specs=[vmem] * 2,
        out_shape=[half, half],
        compiler_params=pltpu.CompilerParams(vmem_limit_bytes=8 * 2**20),
        name="halve",
    )(up, down)


NT = (((1,), (1,)), ((), ()))


def stack_kernel(r0, r1, r2, r3, out_ref):
    for i, ref in enumerate((r0, r1, r2, r3)):
        out_ref[256 * i : 256 * i + 256, :] = ref[...]


def stack(pieces):
    vmem = pl.BlockSpec(memory_space=pltpu.VMEM)
    rows, d = pieces[0].shape
    return pl.pallas_call(
        stack_kernel,
        in_specs=[vmem] * 4,
        out_specs=vmem,
        out_shape=jax.ShapeDtypeStruct((4 * rows, d), jnp.bfloat16),
        compiler_params=pltpu.CompilerParams(vmem_limit_bytes=16 * 2**20),
        name="stack_rows",
    )(*pieces)


def add_products(where, rows, weights, turn, offset, own, other, total, first):
    z = (where[0] + offset + 8) % 8
    r = (z // 2 - where[1] + 4) % 4
    quarter = weights.shape[-1]
    for core, parts in ((where[2], own), (1 - where[2], other)):
        at = 0
        for ref in parts:
            width = ref.shape[1]
            for m in range(3):
                for g in range(3):
                    to = pl.multiple_of((z % 2 * 128 + core * 96 + 32 * g) % 192, 32)
                    low = 96 * m + 32 * g
                    weights[turn, m, pl.ds(to, 32), at : at + width] = ref[low : low + 32, :]
            at += width
    for m in range(3):
        weights[turn, m, 192:, :] = jnp.zeros((64, quarter), jnp.bfloat16)
    product = lax.dot_general(
        rows[:, pl.ds(pl.multiple_of(r * quarter, 128), quarter)],
        weights[turn].reshape(768, quarter),
        NT,
        preferred_element_type=jnp.float32,
    )
    if first:
        total[z % 2] = product
    else:
        total[z % 2] = total[z % 2] + product


def project_kernel(offsets, where, rows, *refs):
    pieces, total, weights = refs[: 2 * len(offsets)], refs[-2], refs[-1]
    for turn, offset in enumerate(offsets):
        own, other = [[pieces[2 * turn + side]] for side in range(2)]
        add_products(where, rows, weights, turn, offset, own, other, total, offset in (0, -1))


def project(where, rows, offsets, pieces, before=()):
    vmem = pl.BlockSpec(memory_space=pltpu.VMEM)
    quarter = rows.shape[1] // 4
    return pl.pallas_call(
        lambda *refs: project_kernel(offsets, *refs),
        in_specs=[pl.BlockSpec(memory_space=pltpu.SMEM)] + [vmem] * (1 + len(pieces) + len(before)),
        out_specs=vmem,
        out_shape=jax.ShapeDtypeStruct((2, rows.shape[0], 768), jnp.float32),
        scratch_shapes=[pltpu.VMEM((len(offsets), 3, 256, quarter), jnp.bfloat16)],
        input_output_aliases={2 + len(pieces): 0} if before else {},
        compiler_params=pltpu.CompilerParams(vmem_limit_bytes=20 * 2**20),
        name="project",
    )(where, rows, *pieces, *before)


def head_columns(total, rows, m, h):
    at = 256 * m
    if h == 0:
        return total[0, rows, at : at + 128]
    if h == 2:
        return total[1, rows, at : at + 128]
    return jnp.concatenate([total[half, rows, at + 128 : at + 192] for half in range(2)], axis=-1)


def attend_kernel(where, rows, fh, fho, bh, bho, qg_ref, kg_ref, before, out_ref, weights, total):
    total[...] = before[...]
    add_products(where, rows, weights, 0, 4, [fh, bh], [fho, bho], total, False)

    @pl.when(where[0] >= 0)
    def _():
        gains = qg_ref[...] * kg_ref[...] * (128.0**-0.5)
        row_patch = lax.broadcasted_iota(jnp.int32, (256, 256), 0) % 8
        col_patch = lax.broadcasted_iota(jnp.int32, (256, 256), 1) % 8
        same = row_patch == col_patch
        for i in range(4):
            part = slice(256 * i, 256 * i + 256)
            for h in range(3):
                q_rows = head_columns(total, part, 0, h).astype(jnp.bfloat16)
                k = head_columns(total, part, 1, h).astype(jnp.bfloat16).astype(jnp.float32)
                v = head_columns(total, part, 2, h).astype(jnp.bfloat16)
                q = q_rows.astype(jnp.float32)
                q_scale = lax.rsqrt(jnp.mean(q * q, axis=-1, keepdims=True) + 1e-06)
                k_scale = lax.rsqrt(jnp.mean(k * k, axis=-1, keepdims=True) + 1e-06)
                k_unit = (k * k_scale * gains).astype(jnp.bfloat16)
                scores = lax.dot_general(q_rows, k_unit, NT, preferred_element_type=jnp.float32)
                exps = jnp.where(same, jnp.exp(scores * q_scale), 0.0)
                probs = (exps / jnp.sum(exps, axis=-1, keepdims=True)).astype(jnp.bfloat16)
                out = jnp.dot(probs, v, preferred_element_type=jnp.float32).astype(jnp.bfloat16)
                out_ref[:, 16 * i : 16 * i + 16, 128 * h : 128 * h + 128] = out.reshape(16, 16, 128)


def attend(where, rows, pieces, query_gain, key_gain, before):
    vmem = pl.BlockSpec(memory_space=pltpu.VMEM)
    quarter = rows.shape[1] // 4
    return pl.pallas_call(
        attend_kernel,
        in_specs=[pl.BlockSpec(memory_space=pltpu.SMEM)] + [vmem] * (4 + len(pieces)),
        out_specs=vmem,
        scratch_shapes=[
            pltpu.VMEM((1, 3, 256, quarter), jnp.bfloat16),
            pltpu.VMEM((2, rows.shape[0], 768), jnp.float32),
        ],
        out_shape=jax.ShapeDtypeStruct((16, 64, 384), jnp.bfloat16),
        compiler_params=pltpu.CompilerParams(vmem_limit_bytes=28 * 2**20),
        name="project_attend",
    )(where, rows, *pieces, query_gain.reshape(1, 128), key_gain.reshape(1, 128), before)


def sources(core):
    found = {}
    for x in range(4):
        for y in range(4):
            for piece, shift in enumerate(SHIFTS):
                s = ((x - shift) % 4) * 4 + y if core == 0 else x * 4 + (y - shift) % 4
                found[s, (x + y) % 4] = (4 * x + y, piece)
    return found


def assemble_kernel(core_ref, recv_ref, out_ref):
    for core in range(2):

        @pl.when(core_ref[0] == core)
        def _(found=sources(core)):
            for s in range(0, 16, 2):
                for j in range(4):
                    src, piece = found[s, j]
                    low = recv_ref[src, 16 * piece : 16 * piece + 16, :].astype(jnp.float32)
                    src, piece = found[s + 1, j]
                    high = recv_ref[src, 16 * piece : 16 * piece + 16, :].astype(jnp.float32)
                    for f in range(2):
                        both = jnp.concatenate([low[8 * f : 8 * f + 8], high[8 * f : 8 * f + 8]], axis=0)
                        out_ref[0, f, 8 * s : 8 * s + 16, 384 * j : 384 * j + 384] = both.astype(jnp.bfloat16)


def assemble(received, core):
    return pl.pallas_call(
        assemble_kernel,
        in_specs=[pl.BlockSpec(memory_space=pltpu.SMEM), pl.BlockSpec(memory_space=pltpu.VMEM)],
        out_specs=pl.BlockSpec(memory_space=pltpu.VMEM),
        out_shape=jax.ShapeDtypeStruct((1, 2, 128, 1536), jnp.bfloat16),
        compiler_params=pltpu.CompilerParams(vmem_limit_bytes=40 * 2**20),
        name="assemble_heads",
    )(core, received)


def shards(video, norm_gain, w_query, w_key, w_value, query_gain, key_gain):
    seq = lax.axis_index("seq")
    fsdp = lax.axis_index("fsdp")
    z = lax.axis_index("dp") * 4 + fsdp // 2
    core = (fsdp % 2).astype(jnp.int32).reshape(1)
    group = (seq // 4 + seq % 4) % 4
    where = jnp.stack([z, group, fsdp % 2]).astype(jnp.int32)
    d = video.shape[-1]
    quarter = d // 4

    quarters = pack([w.T for w in (w_query, w_key, w_value)])
    with jax.named_scope("scatter"):
        far, one, three = [lax.ppermute(quarters[r], AXES, scatter_perm(r)) for r in (2, 1, 3)]
    part = choose(where, [quarters[0], one, far, three])

    normed = layer_normed(video, norm_gain)
    with jax.named_scope("rows_home"):
        home = lax.all_to_all(normed, "seq", split_axis=0, concat_axis=0, tiled=True).reshape(256, d)
    with jax.named_scope("rows_line"):
        rows = stack([home] + [lax.ppermute(home, AXES, line_perm(s)) for s in SHIFTS[1:]])

    def swapped(piece):
        with jax.named_scope("swap"):
            return piece, lax.ppermute(piece, AXES, swap_perm())

    with jax.named_scope("ring"):
        ups, downs = [part], [part]
        for _ in range(3):
            ups.append(lax.ppermute(ups[-1], AXES, ring_perm(1)))
            downs.append(lax.ppermute(downs[-1], AXES, ring_perm(-1)))
        ups[3], downs[3], rows = lax.optimization_barrier((ups[3], downs[3], rows))
        up_half, down_half = halve(ups[3], downs[3])
        up_half = lax.ppermute(up_half, AXES, ring_perm(1))
        down_half = lax.ppermute(down_half, AXES, ring_perm(-1))
    early = swapped(part) + swapped(ups[1]) + swapped(downs[1]) + swapped(ups[2]) + swapped(downs[2])
    total = project(where, rows, (0, -1, 1, -2, 2), early)
    total = project(where, rows, (-3, 3), swapped(ups[3]) + swapped(downs[3]), (total,))
    up_half, down_half, total = lax.optimization_barrier((up_half, down_half, total))
    late = swapped(up_half) + swapped(down_half)
    output = attend(where, rows, late, query_gain, key_gain, total)
    with jax.named_scope("heads_back"):
        received = lax.all_to_all(output, "seq", split_axis=0, concat_axis=0, tiled=True)
    return assemble(received, core)


def solution(mesh):
    in_specs = (
        P(("dp", "fsdp"), "seq", None, None),
        P(),
        P(None, ("dp", "fsdp")),
        P(None, ("dp", "fsdp")),
        P(None, ("dp", "fsdp")),
        P(),
        P(),
    )
    out_specs = P(("dp", "fsdp"), "seq", None, None)
    return jax.shard_map(shards, mesh=mesh, in_specs=in_specs, out_specs=out_specs, check_vma=False)
```

```python
import jax
import jax.numpy as jnp
from jax import lax
from jax.experimental import pallas as pl
from jax.experimental.pallas import tpu as pltpu
from jax.sharding import PartitionSpec as P

AXES = ("dp", "seq", "fsdp")
SHIFTS = (0, 1, 3, 2)


def place(x, y, z, core):
    return ((z // 4) * 16 + x * 4 + y) * 8 + (z % 4) * 2 + core


def every_place():
    return [(x, y, z, c) for x in range(4) for y in range(4) for z in range(8) for c in range(2)]


def scatter_perm(shift):
    pairs = []
    for x in range(4):
        for y in range(4):
            j = (x + y) % 4
            origin = (x + 2) % 4 if shift == 2 else x
            for a in range(2):
                for c in range(2):
                    z = 2 * j + a
                    pairs.append((place(origin, y, z, c), place(x, y, (z + 2 * shift) % 8, c)))
    return pairs


def line_perm(shift):
    pairs = []
    for x, y, z, c in every_place():
        to = ((x + shift) % 4, y) if c == 0 else (x, (y + shift) % 4)
        pairs.append((place(x, y, z, c), place(to[0], to[1], z, c)))
    return pairs


def cross_perm(shift):
    pairs = []
    for x, y, z, c in every_place():
        to = (x, (y + shift) % 4) if c == 0 else ((x + shift) % 4, y)
        pairs.append((place(x, y, z, c), place(to[0], to[1], z, c)))
    return pairs


def ring_perm(step):
    return [(place(x, y, z, c), place(x, y, (z + step) % 8, c)) for x, y, z, c in every_place()]


def swap_perm():
    return [(place(x, y, z, c), place(x, y, z, 1 - c)) for x, y, z, c in every_place()]


def prepare_kernel(where, video, wq, wk, wv, f0, f1, f2, f3, q0, q1, q2, q3, frames, columns, packed, sems, out_sems):
    cross = jnp.where(where[2] == 0, where[4], where[3])
    step, height, quarter = frames.shape[2], columns.shape[1], packed.shape[2]
    fetch_columns = [pltpu.make_async_copy(w, columns.at[m], sems.at[m]) for m, w in enumerate((wq, wk, wv))]
    fetch_frames = []
    for s in range(4):
        at = pl.multiple_of((cross + s) % 4 * step, step)
        fetch_frames.append(
            pltpu.make_async_copy(video.at[0, :, pl.ds(at, step), :], frames.at[s], sems.at[3 + s])
        )
    for copy in fetch_columns + fetch_frames:
        copy.start()
    stores = []
    for copy in fetch_columns:
        copy.wait()
    for r, out in ((2, q2), (1, q1), (3, q3), (0, q0)):
        for m in range(3):
            packed[r, height * m : height * (m + 1), :] = columns[m, :, quarter * r : quarter * (r + 1)]
        stores.append(pltpu.make_async_copy(packed.at[r], out, out_sems.at[r]))
        stores[-1].start()
    for s, out in enumerate((f0, f1, f2, f3)):
        fetch_frames[s].wait()
        stores.append(pltpu.make_async_copy(frames.at[s], out, out_sems.at[4 + s]))
        stores[-1].start()
    for store in stores:
        store.wait()


def prepare(where, video, columns):
    _, frames, patches, d = video.shape
    height = columns[0].shape[0]
    anywhere = pl.BlockSpec(memory_space=pl.ANY)
    return pl.pallas_call(
        prepare_kernel,
        in_specs=[pl.BlockSpec(memory_space=pltpu.SMEM)] + [anywhere] * 4,
        out_specs=[anywhere] * 8,
        out_shape=[jax.ShapeDtypeStruct((frames, patches // 4, d), jnp.bfloat16)] * 4
        + [jax.ShapeDtypeStruct((3 * height, d // 4), jnp.bfloat16)] * 4,
        scratch_shapes=[
            pltpu.VMEM((4, frames, patches // 4, d), jnp.bfloat16),
            pltpu.VMEM((3, height, d), jnp.bfloat16),
            pltpu.VMEM((4, 3 * height, d // 4), jnp.bfloat16),
            pltpu.SemaphoreType.DMA((7,)),
            pltpu.SemaphoreType.DMA((8,)),
        ],
        compiler_params=pltpu.CompilerParams(vmem_limit_bytes=60 * 2**20),
        name="prepare",
    )(where, video, *columns)


def norm_kernel(f0, f1, f2, f3, gain, out):
    at = 0
    for ref in (f0, f1, f2, f3):
        for f in range(ref.shape[0]):
            values = ref[f].astype(jnp.float32)
            average = jnp.mean(values, axis=-1, keepdims=True)
            centred = values - average
            spread = jnp.mean(centred * centred, axis=-1, keepdims=True)
            normed = centred * lax.rsqrt(spread + 1e-06) * gain[...]
            out[at : at + ref.shape[1], :] = normed.astype(jnp.bfloat16)
            at += ref.shape[1]


def layer_normed(blocks, gain):
    vmem = pl.BlockSpec(memory_space=pltpu.VMEM)
    frames, patches, d = blocks[0].shape
    return pl.pallas_call(
        norm_kernel,
        in_specs=[vmem] * 5,
        out_specs=vmem,
        out_shape=jax.ShapeDtypeStruct((4 * frames * patches, d), jnp.bfloat16),
        compiler_params=pltpu.CompilerParams(vmem_limit_bytes=10 * 2**20),
        name="norm_rows",
    )(*blocks, gain.reshape(1, d))


def choose_kernel(where, q0, q1, q2, q3, out_ref, sem):
    quarter = (where[0] // 2 - where[1] + 4) % 4
    for r, ref in enumerate((q0, q1, q2, q3)):

        @pl.when(quarter == r)
        def _(ref=ref):
            copy = pltpu.make_async_copy(ref, out_ref, sem)
            copy.start()
            copy.wait()


def choose(where, parts):
    anywhere = pl.BlockSpec(memory_space=pl.ANY)
    return pl.pallas_call(
        choose_kernel,
        in_specs=[pl.BlockSpec(memory_space=pltpu.SMEM)] + [anywhere] * 4,
        out_specs=anywhere,
        out_shape=jax.ShapeDtypeStruct(parts[0].shape, parts[0].dtype),
        scratch_shapes=[pltpu.SemaphoreType.DMA],
        compiler_params=pltpu.CompilerParams(vmem_limit_bytes=4 * 2**20),
        name="choose_quarter",
    )(where, *parts)


def halve_kernel(up, down, up_half, down_half):
    width = up_half.shape[1]
    up_half[...] = up[:, :width]
    down_half[...] = down[:, width:]


def halve(up, down):
    vmem = pl.BlockSpec(memory_space=pltpu.VMEM)
    half = jax.ShapeDtypeStruct((up.shape[0], up.shape[1] // 2), up.dtype)
    return pl.pallas_call(
        halve_kernel,
        in_specs=[vmem] * 2,
        out_specs=[vmem] * 2,
        out_shape=[half, half],
        compiler_params=pltpu.CompilerParams(vmem_limit_bytes=8 * 2**20),
        name="halve",
    )(up, down)


NT = (((1,), (1,)), ((), ()))


def stack_kernel(r0, r1, r2, r3, out_ref):
    for i, ref in enumerate((r0, r1, r2, r3)):
        out_ref[256 * i : 256 * i + 256, :] = ref[...]


def stack(pieces):
    vmem = pl.BlockSpec(memory_space=pltpu.VMEM)
    rows, d = pieces[0].shape
    return pl.pallas_call(
        stack_kernel,
        in_specs=[vmem] * 4,
        out_specs=vmem,
        out_shape=jax.ShapeDtypeStruct((4 * rows, d), jnp.bfloat16),
        compiler_params=pltpu.CompilerParams(vmem_limit_bytes=16 * 2**20),
        name="stack_rows",
    )(*pieces)


def add_products(where, rows, weights, turn, offset, own, other, total, first):
    z = (where[0] + offset + 8) % 8
    r = (z // 2 - where[1] + 4) % 4
    quarter = weights.shape[-1]
    for core, parts in ((where[2], own), (1 - where[2], other)):
        at = 0
        for ref in parts:
            width = ref.shape[1]
            for m in range(3):
                for g in range(3):
                    to = pl.multiple_of((z % 2 * 128 + core * 96 + 32 * g) % 192, 32)
                    low = 96 * m + 32 * g
                    weights[turn, m, pl.ds(to, 32), at : at + width] = ref[low : low + 32, :]
            at += width
    for m in range(3):
        weights[turn, m, 192:, :] = jnp.zeros((64, quarter), jnp.bfloat16)
    product = lax.dot_general(
        rows[:, pl.ds(pl.multiple_of(r * quarter, 128), quarter)],
        weights[turn].reshape(768, quarter),
        NT,
        preferred_element_type=jnp.float32,
    )
    product = product.reshape(total.shape[1:])
    if first:
        total[z % 2] = product
    else:
        total[z % 2] = total[z % 2] + product


def project_kernel(offsets, where, rows, *refs):
    pieces, total, weights = refs[: 2 * len(offsets)], refs[-2], refs[-1]
    for turn, offset in enumerate(offsets):
        own, other = [[pieces[2 * turn + side]] for side in range(2)]
        add_products(where, rows, weights, turn, offset, own, other, total, offset in (0, -1))


def project(where, rows, offsets, pieces, before=()):
    vmem = pl.BlockSpec(memory_space=pltpu.VMEM)
    quarter = rows.shape[1] // 4
    return pl.pallas_call(
        lambda *refs: project_kernel(offsets, *refs),
        in_specs=[pl.BlockSpec(memory_space=pltpu.SMEM)] + [vmem] * (1 + len(pieces) + len(before)),
        out_specs=vmem,
        out_shape=jax.ShapeDtypeStruct((2, 32, 4, 8, 768), jnp.float32),
        scratch_shapes=[pltpu.VMEM((len(offsets), 3, 256, quarter), jnp.bfloat16)],
        input_output_aliases={2 + len(pieces): 0} if before else {},
        compiler_params=pltpu.CompilerParams(vmem_limit_bytes=20 * 2**20),
        name="project",
    )(where, rows, *pieces, *before)


def head_columns(total, g, m, h):
    at = 256 * m
    if h == 1:
        halves = [total[half, :, g, :, at + 128 : at + 192] for half in range(2)]
        return jnp.concatenate(halves, axis=-1).reshape(256, 128)
    return total[h // 2, :, g, :, at : at + 128].reshape(256, 128)


def attend_kernel(where, rows, fh, fho, bh, bho, qg_ref, kg_ref, before, out_ref, weights, total, found):
    total[...] = before[...]
    add_products(where, rows, weights, 0, 4, [fh, bh], [fho, bho], total, False)

    @pl.when(where[0] >= 0)
    def _():
        gains = qg_ref[...] * kg_ref[...] * (128.0**-0.5)
        row_patch = lax.broadcasted_iota(jnp.int32, (256, 256), 0) % 8
        col_patch = lax.broadcasted_iota(jnp.int32, (256, 256), 1) % 8
        same = row_patch == col_patch
        for g in range(4):
            for h in range(3):
                q_rows = head_columns(total, g, 0, h).astype(jnp.bfloat16)
                k = head_columns(total, g, 1, h).astype(jnp.bfloat16).astype(jnp.float32)
                v = head_columns(total, g, 2, h).astype(jnp.bfloat16)
                q = q_rows.astype(jnp.float32)
                q_scale = lax.rsqrt(jnp.mean(q * q, axis=-1, keepdims=True) + 1e-06)
                k_scale = lax.rsqrt(jnp.mean(k * k, axis=-1, keepdims=True) + 1e-06)
                k_unit = (k * k_scale * gains).astype(jnp.bfloat16)
                scores = lax.dot_general(q_rows, k_unit, NT, preferred_element_type=jnp.float32)
                exps = jnp.where(same, jnp.exp(scores * q_scale), 0.0)
                probs = (exps / jnp.sum(exps, axis=-1, keepdims=True)).astype(jnp.bfloat16)
                out = jnp.dot(probs, v, preferred_element_type=jnp.float32)
                found[:, g, :, 128 * h : 128 * h + 128] = out.reshape(32, 8, 128)
        core = where[2]
        along = jnp.where(core == 0, where[3], where[4])
        cross = jnp.where(core == 0, where[4], where[3])
        for piece, shift in enumerate(SHIFTS):
            for s in range(4):
                line, side = (along - shift + 4) % 4, (cross - s + 4) % 4
                to = jnp.where(core == 0, 4 * line + side, 4 * side + line)
                frame = 8 * piece + 2 * s
                out_ref[to] = found[frame : frame + 2].reshape(64, 384).astype(jnp.bfloat16)


def attend(where, rows, pieces, query_gain, key_gain, before):
    vmem = pl.BlockSpec(memory_space=pltpu.VMEM)
    quarter = rows.shape[1] // 4
    return pl.pallas_call(
        attend_kernel,
        in_specs=[pl.BlockSpec(memory_space=pltpu.SMEM)] + [vmem] * (4 + len(pieces)),
        out_specs=vmem,
        scratch_shapes=[
            pltpu.VMEM((1, 3, 256, quarter), jnp.bfloat16),
            pltpu.VMEM((2, 32, 4, 8, 768), jnp.float32),
            pltpu.VMEM((32, 4, 8, 384), jnp.float32),
        ],
        out_shape=jax.ShapeDtypeStruct((16, 64, 384), jnp.bfloat16),
        compiler_params=pltpu.CompilerParams(vmem_limit_bytes=30 * 2**20),
        name="project_attend",
    )(where, rows, *pieces, query_gain.reshape(1, 128), key_gain.reshape(1, 128), before)


def assemble_kernel(where, recv_ref, out_ref):
    for core in range(2):

        @pl.when(where[2] == core)
        def _(core=core):
            for x in range(4):
                for y in range(4):
                    at, j = 32 * (y if core == 0 else x), (x + y) % 4
                    for f in range(2):
                        out_ref[0, f, at : at + 32, 384 * j : 384 * j + 384] = recv_ref[
                            4 * x + y, 32 * f : 32 * f + 32, :
                        ]


def assemble(received, where):
    return pl.pallas_call(
        assemble_kernel,
        in_specs=[pl.BlockSpec(memory_space=pltpu.SMEM), pl.BlockSpec(memory_space=pltpu.VMEM)],
        out_specs=pl.BlockSpec(memory_space=pltpu.VMEM),
        out_shape=jax.ShapeDtypeStruct((1, 2, 128, 1536), jnp.bfloat16),
        compiler_params=pltpu.CompilerParams(vmem_limit_bytes=40 * 2**20),
        name="assemble_heads",
    )(where, received)


def shards(video, norm_gain, w_query, w_key, w_value, query_gain, key_gain):
    seq = lax.axis_index("seq")
    fsdp = lax.axis_index("fsdp")
    z = lax.axis_index("dp") * 4 + fsdp // 2
    group = (seq // 4 + seq % 4) % 4
    where = jnp.stack([z, group, fsdp % 2, seq // 4, seq % 4]).astype(jnp.int32)

    *blocks, q0, q1, q2, q3 = prepare(where, video, [w.T for w in (w_query, w_key, w_value)])
    with jax.named_scope("rows_cross"):
        blocks = [blocks[0]] + [lax.ppermute(blocks[s], AXES, cross_perm(s)) for s in (1, 2, 3)]
    with jax.named_scope("scatter"):
        q2, q1, q3 = [lax.ppermute(q, AXES, scatter_perm(r)) for r, q in ((2, q2), (1, q1), (3, q3))]
    part = choose(where, [q0, q1, q2, q3])

    home = layer_normed(blocks, norm_gain)
    with jax.named_scope("rows_line"):
        rows = stack([home] + [lax.ppermute(home, AXES, line_perm(s)) for s in SHIFTS[1:]])

    def swapped(piece):
        with jax.named_scope("swap"):
            return piece, lax.ppermute(piece, AXES, swap_perm())

    def onward(up, down):
        with jax.named_scope("ring"):
            return lax.ppermute(up, AXES, ring_perm(1)), lax.ppermute(down, AXES, ring_perm(-1))

    up1, down1 = onward(part, part)
    up2, down2 = onward(up1, down1)
    up3, down3 = onward(up2, down2)
    early = swapped(part) + swapped(up1) + swapped(down1) + swapped(up2) + swapped(down2)
    total = project(where, rows, (0, -1, 1, -2, 2), early)
    up3, down3, total = lax.optimization_barrier((up3, down3, total))
    up4, down4 = onward(*halve(up3, down3))
    total = project(where, rows, (-3, 3), swapped(up3) + swapped(down3), (total,))
    up4, down4, total = lax.optimization_barrier((up4, down4, total))
    output = attend(where, rows, swapped(up4) + swapped(down4), query_gain, key_gain, total)
    with jax.named_scope("heads_back"):
        received = lax.all_to_all(output, "seq", split_axis=0, concat_axis=0, tiled=True)
    return assemble(received, where)


def solution(mesh):
    in_specs = (
        P(("dp", "fsdp"), "seq", None, None),
        P(),
        P(None, ("dp", "fsdp")),
        P(None, ("dp", "fsdp")),
        P(None, ("dp", "fsdp")),
        P(),
        P(),
    )
    out_specs = P(("dp", "fsdp"), "seq", None, None)
    return jax.shard_map(shards, mesh=mesh, in_specs=in_specs, out_specs=out_specs, check_vma=False)
```

```python
import jax
import jax.numpy as jnp
from jax import lax
from jax.experimental import pallas as pl
from jax.experimental.pallas import tpu as pltpu
from jax.sharding import PartitionSpec as P

AXES = ("dp", "seq", "fsdp")
SHIFTS = (0, 1, 3, 2)
CHOOSE_COST = 9_000_000_000


def place(x, y, z, core):
    return ((z // 4) * 16 + x * 4 + y) * 8 + (z % 4) * 2 + core


def every_place():
    return [(x, y, z, c) for x in range(4) for y in range(4) for z in range(8) for c in range(2)]


def scatter_perm(shift):
    pairs = []
    for x in range(4):
        for y in range(4):
            j = (x + y) % 4
            origin = (x + 2) % 4 if shift == 2 else x
            for a in range(2):
                for c in range(2):
                    z = 2 * j + a
                    pairs.append((place(origin, y, z, c), place(x, y, (z + 2 * shift) % 8, c)))
    return pairs


def line_perm(shift):
    pairs = []
    for x, y, z, c in every_place():
        to = ((x + shift) % 4, y) if c == 0 else (x, (y + shift) % 4)
        pairs.append((place(x, y, z, c), place(to[0], to[1], z, c)))
    return pairs


def cross_perm(shift):
    pairs = []
    for x, y, z, c in every_place():
        to = (x, (y + shift) % 4) if c == 0 else ((x + shift) % 4, y)
        pairs.append((place(x, y, z, c), place(to[0], to[1], z, c)))
    return pairs


def ring_perm(step):
    return [(place(x, y, z, c), place(x, y, (z + step) % 8, c)) for x, y, z, c in every_place()]


def partner_perm(side):
    pairs = []
    for x, y, z, c in every_place():
        step = side * (1 - 2 * (x % 2))
        pairs.append((place(x, y, z, c), place((x + step) % 4, (y - step) % 4, z, c)))
    return pairs


def swap_perm():
    return [(place(x, y, z, c), place(x, y, z, 1 - c)) for x, y, z, c in every_place()]


def prepare_kernel(where, video, wq, wk, wv, f0, f1, f2, f3, q0, q1, q2, q3, frames, columns, packed, sems, out_sems):
    cross = jnp.where(where[2] == 0, where[4], where[3])
    step, height, quarter = frames.shape[2], columns.shape[1], packed.shape[2]
    fetch_columns = [pltpu.make_async_copy(w, columns.at[m], sems.at[m]) for m, w in enumerate((wq, wk, wv))]
    fetch_frames = []
    for s in range(4):
        at = pl.multiple_of((cross + s) % 4 * step, step)
        fetch_frames.append(
            pltpu.make_async_copy(video.at[0, :, pl.ds(at, step), :], frames.at[s], sems.at[3 + s])
        )
    for copy in fetch_columns + fetch_frames:
        copy.start()
    stores = []
    for copy in fetch_columns:
        copy.wait()
    for r, out in ((2, q2), (1, q1), (3, q3), (0, q0)):
        for m in range(3):
            at = pl.multiple_of((r + 2 * where[6]) % 4 * quarter, 128)
            packed[r, height * m : height * (m + 1), :] = columns[m, :, pl.ds(at, quarter)]
        stores.append(pltpu.make_async_copy(packed.at[r], out, out_sems.at[r]))
        stores[-1].start()
    for s, out in enumerate((f0, f1, f2, f3)):
        fetch_frames[s].wait()
        stores.append(pltpu.make_async_copy(frames.at[s], out, out_sems.at[4 + s]))
        stores[-1].start()
    for store in stores:
        store.wait()


def prepare(where, video, columns):
    _, frames, patches, d = video.shape
    height = columns[0].shape[0]
    anywhere = pl.BlockSpec(memory_space=pl.ANY)
    return pl.pallas_call(
        prepare_kernel,
        in_specs=[pl.BlockSpec(memory_space=pltpu.SMEM)] + [anywhere] * 4,
        out_specs=[anywhere] * 8,
        out_shape=[jax.ShapeDtypeStruct((frames, patches // 4, d), jnp.bfloat16)] * 4
        + [jax.ShapeDtypeStruct((3 * height, d // 4), jnp.bfloat16)] * 4,
        scratch_shapes=[
            pltpu.VMEM((4, frames, patches // 4, d), jnp.bfloat16),
            pltpu.VMEM((3, height, d), jnp.bfloat16),
            pltpu.VMEM((4, 3 * height, d // 4), jnp.bfloat16),
            pltpu.SemaphoreType.DMA((7,)),
            pltpu.SemaphoreType.DMA((8,)),
        ],
        compiler_params=pltpu.CompilerParams(vmem_limit_bytes=60 * 2**20),
        name="prepare",
    )(where, video, *columns)


def norm_kernel(f0, f1, f2, f3, gain, out):
    at = 0
    for ref in (f0, f1, f2, f3):
        for f in range(ref.shape[0]):
            values = ref[f].astype(jnp.float32)
            average = jnp.mean(values, axis=-1, keepdims=True)
            centred = values - average
            spread = jnp.mean(centred * centred, axis=-1, keepdims=True)
            normed = centred * lax.rsqrt(spread + 1e-06) * gain[...]
            out[at : at + ref.shape[1], :] = normed.astype(jnp.bfloat16)
            at += ref.shape[1]


def layer_normed(blocks, gain):
    vmem = pl.BlockSpec(memory_space=pltpu.VMEM)
    frames, patches, d = blocks[0].shape
    return pl.pallas_call(
        norm_kernel,
        in_specs=[vmem] * 5,
        out_specs=vmem,
        out_shape=jax.ShapeDtypeStruct((4 * frames * patches, d), jnp.bfloat16),
        compiler_params=pltpu.CompilerParams(vmem_limit_bytes=10 * 2**20),
        name="norm_rows",
    )(*blocks, gain.reshape(1, d))


def choose_kernel(where, q0, q1, q2, q3, out_ref, sem):
    quarter = (where[5] // 2 - where[1] + 4) % 4
    for r, ref in enumerate((q0, q1, q2, q3)):

        @pl.when(quarter == r)
        def _(ref=ref):
            copy = pltpu.make_async_copy(ref, out_ref, sem)
            copy.start()
            copy.wait()


def choose(where, parts):
    anywhere = pl.BlockSpec(memory_space=pl.ANY)
    return pl.pallas_call(
        choose_kernel,
        in_specs=[pl.BlockSpec(memory_space=pltpu.SMEM)] + [anywhere] * 4,
        out_specs=anywhere,
        out_shape=jax.ShapeDtypeStruct(parts[0].shape, parts[0].dtype),
        scratch_shapes=[pltpu.SemaphoreType.DMA],
        cost_estimate=pl.CostEstimate(flops=CHOOSE_COST, bytes_accessed=2**20, transcendentals=0),
        compiler_params=pltpu.CompilerParams(vmem_limit_bytes=4 * 2**20),
        name="choose_quarter",
    )(where, *parts)


NT = (((1,), (1,)), ((), ()))


def stack_kernel(r0, r1, r2, r3, out_ref):
    for i, ref in enumerate((r0, r1, r2, r3)):
        out_ref[256 * i : 256 * i + 256, :] = ref[...]


def stack(pieces):
    vmem = pl.BlockSpec(memory_space=pltpu.VMEM)
    rows, d = pieces[0].shape
    return pl.pallas_call(
        stack_kernel,
        in_specs=[vmem] * 4,
        out_specs=vmem,
        out_shape=jax.ShapeDtypeStruct((4 * rows, d), jnp.bfloat16),
        compiler_params=pltpu.CompilerParams(vmem_limit_bytes=16 * 2**20),
        name="stack_rows",
    )(*pieces)


def add_products(where, rows, weights, turn, offset, own, other, total, first):
    z = (where[0] + offset + 8) % 8
    r = (z // 2 - where[1] + 4) % 4
    quarter = weights.shape[-1]
    for core, ref in ((where[2], own), (1 - where[2], other)):
        for m in range(3):
            for g in range(3):
                to = pl.multiple_of((z % 2 * 128 + core * 96 + 32 * g) % 192, 32)
                low = 96 * m + 32 * g
                weights[turn, m, pl.ds(to, 32), :] = ref[low : low + 32, :]
    for m in range(3):
        weights[turn, m, 192:, :] = jnp.zeros((64, quarter), jnp.bfloat16)
    product = lax.dot_general(
        rows[:, pl.ds(pl.multiple_of(r * quarter, 128), quarter)],
        weights[turn].reshape(768, quarter),
        NT,
        preferred_element_type=jnp.float32,
    )
    product = product.reshape(total.shape[1:])
    if first:
        total[z % 2] = product
    else:
        total[z % 2] = total[z % 2] + product


def project_kernel(offsets, where, rows, *refs):
    pieces, total, weights = refs[: 2 * len(offsets)], refs[-2], refs[-1]
    for turn, offset in enumerate(offsets):
        own, other = pieces[2 * turn], pieces[2 * turn + 1]
        add_products(where, rows, weights, turn, offset, own, other, total, offset in (0, -1))


def project(where, rows, offsets, pieces, before=()):
    vmem = pl.BlockSpec(memory_space=pltpu.VMEM)
    quarter = rows.shape[1] // 4
    return pl.pallas_call(
        lambda *refs: project_kernel(offsets, *refs),
        in_specs=[pl.BlockSpec(memory_space=pltpu.SMEM)] + [vmem] * (1 + len(pieces) + len(before)),
        out_specs=vmem,
        out_shape=jax.ShapeDtypeStruct((2, 32, 4, 8, 768), jnp.float32),
        scratch_shapes=[pltpu.VMEM((len(offsets), 3, 256, quarter), jnp.bfloat16)],
        input_output_aliases={2 + len(pieces): 0} if before else {},
        compiler_params=pltpu.CompilerParams(vmem_limit_bytes=20 * 2**20),
        name="project",
    )(where, rows, *pieces, *before)


def head_columns(total, g, m, h):
    at = 256 * m
    if h == 1:
        halves = [total[half, :, g, :, at + 128 : at + 192] for half in range(2)]
        return jnp.concatenate(halves, axis=-1).reshape(256, 128)
    return total[h // 2, :, g, :, at : at + 128].reshape(256, 128)


def attend_kernel(where, rows, *refs):
    pieces, (qg_ref, kg_ref, before, out_ref, weights, total, found) = refs[:6], refs[6:]
    total[...] = before[...]
    for turn, offset in enumerate((-3, 3, 4)):
        add_products(where, rows, weights, turn, offset, pieces[2 * turn], pieces[2 * turn + 1], total, False)

    @pl.when(where[0] >= 0)
    def _():
        gains = qg_ref[...] * kg_ref[...] * (128.0**-0.5)
        row_patch = lax.broadcasted_iota(jnp.int32, (256, 256), 0) % 8
        col_patch = lax.broadcasted_iota(jnp.int32, (256, 256), 1) % 8
        same = row_patch == col_patch
        for g in range(4):
            for h in range(3):
                q_rows = head_columns(total, g, 0, h).astype(jnp.bfloat16)
                k = head_columns(total, g, 1, h).astype(jnp.bfloat16).astype(jnp.float32)
                v = head_columns(total, g, 2, h).astype(jnp.bfloat16)
                q = q_rows.astype(jnp.float32)
                q_scale = lax.rsqrt(jnp.mean(q * q, axis=-1, keepdims=True) + 1e-06)
                k_scale = lax.rsqrt(jnp.mean(k * k, axis=-1, keepdims=True) + 1e-06)
                k_unit = (k * k_scale * gains).astype(jnp.bfloat16)
                scores = lax.dot_general(q_rows, k_unit, NT, preferred_element_type=jnp.float32)
                exps = jnp.where(same, jnp.exp(scores * q_scale), 0.0)
                probs = (exps / jnp.sum(exps, axis=-1, keepdims=True)).astype(jnp.bfloat16)
                out = jnp.dot(probs, v, preferred_element_type=jnp.float32)
                found[:, g, :, 128 * h : 128 * h + 128] = out.reshape(32, 8, 128)
        core = where[2]
        along = jnp.where(core == 0, where[3], where[4])
        cross = jnp.where(core == 0, where[4], where[3])
        for piece, shift in enumerate(SHIFTS):
            for s in range(4):
                line, side = (along - shift + 4) % 4, (cross - s + 4) % 4
                to = jnp.where(core == 0, 4 * line + side, 4 * side + line)
                frame = 8 * piece + 2 * s
                out_ref[to] = found[frame : frame + 2].reshape(64, 384).astype(jnp.bfloat16)


def attend(where, rows, pieces, query_gain, key_gain, before):
    vmem = pl.BlockSpec(memory_space=pltpu.VMEM)
    quarter = rows.shape[1] // 4
    return pl.pallas_call(
        attend_kernel,
        in_specs=[pl.BlockSpec(memory_space=pltpu.SMEM)] + [vmem] * (4 + len(pieces)),
        out_specs=vmem,
        scratch_shapes=[
            pltpu.VMEM((3, 3, 256, quarter), jnp.bfloat16),
            pltpu.VMEM((2, 32, 4, 8, 768), jnp.float32),
            pltpu.VMEM((32, 4, 8, 384), jnp.float32),
        ],
        out_shape=jax.ShapeDtypeStruct((16, 64, 384), jnp.bfloat16),
        compiler_params=pltpu.CompilerParams(vmem_limit_bytes=30 * 2**20),
        name="project_attend",
    )(where, rows, *pieces, query_gain.reshape(1, 128), key_gain.reshape(1, 128), before)


def assemble_kernel(where, recv_ref, out_ref):
    for core in range(2):

        @pl.when(where[2] == core)
        def _(core=core):
            for x in range(4):
                for y in range(4):
                    at, j = 32 * (y if core == 0 else x), (x + y) % 4
                    for f in range(2):
                        out_ref[0, f, at : at + 32, 384 * j : 384 * j + 384] = recv_ref[
                            4 * x + y, 32 * f : 32 * f + 32, :
                        ]


def assemble(received, where):
    return pl.pallas_call(
        assemble_kernel,
        in_specs=[pl.BlockSpec(memory_space=pltpu.SMEM), pl.BlockSpec(memory_space=pltpu.VMEM)],
        out_specs=pl.BlockSpec(memory_space=pltpu.VMEM),
        out_shape=jax.ShapeDtypeStruct((1, 2, 128, 1536), jnp.bfloat16),
        compiler_params=pltpu.CompilerParams(vmem_limit_bytes=40 * 2**20),
        name="assemble_heads",
    )(where, received)


def shards(video, norm_gain, w_query, w_key, w_value, query_gain, key_gain):
    seq = lax.axis_index("seq")
    fsdp = lax.axis_index("fsdp")
    z = lax.axis_index("dp") * 4 + fsdp // 2
    group = (seq // 4 + seq % 4) % 4
    turned = seq // 4 % 2
    where = jnp.stack([(z + 4 * turned) % 8, group, fsdp % 2, seq // 4, seq % 4, z, turned]).astype(jnp.int32)

    *blocks, q0, q1, q2, q3 = prepare(where, video, [w.T for w in (w_query, w_key, w_value)])
    with jax.named_scope("rows_cross"):
        blocks = [blocks[0]] + [lax.ppermute(blocks[s], AXES, cross_perm(s)) for s in (1, 2, 3)]
    with jax.named_scope("scatter"):
        q2, q1, q3 = [lax.ppermute(q, AXES, scatter_perm(r)) for r, q in ((2, q2), (1, q1), (3, q3))]
    part = choose(where, [q0, q1, q2, q3])

    home = layer_normed(blocks, norm_gain)
    with jax.named_scope("rows_line"):
        rows = stack([home] + [lax.ppermute(home, AXES, line_perm(s)) for s in SHIFTS[1:]])

    def swapped(piece):
        with jax.named_scope("swap"):
            return piece, lax.ppermute(piece, AXES, swap_perm())

    def onward(up, down):
        with jax.named_scope("ring"):
            return lax.ppermute(up, AXES, ring_perm(1)), lax.ppermute(down, AXES, ring_perm(-1))

    def partners(piece, side):
        with jax.named_scope("partner"):
            return lax.ppermute(piece, AXES, partner_perm(side))

    up1, down1 = onward(part, part)
    up2, down2 = onward(up1, down1)
    up2, down2, rows = lax.optimization_barrier((up2, down2, rows))
    up3, down3 = onward(up2, down2)
    half_turn = partners(part, 1)
    early = swapped(part) + swapped(up1) + swapped(down1) + swapped(up2) + swapped(down2)
    total = project(where, rows, (0, -1, 1, -2, 2), early)
    up3, down3, half_turn, total = lax.optimization_barrier((up3, down3, half_turn, total))
    late = swapped(up3) + swapped(down3) + swapped(half_turn)
    output = attend(where, rows, late, query_gain, key_gain, total)
    with jax.named_scope("heads_back"):
        received = lax.all_to_all(output, "seq", split_axis=0, concat_axis=0, tiled=True)
    return assemble(received, where)


def solution(mesh):
    in_specs = (
        P(("dp", "fsdp"), "seq", None, None),
        P(),
        P(None, ("dp", "fsdp")),
        P(None, ("dp", "fsdp")),
        P(None, ("dp", "fsdp")),
        P(),
        P(),
    )
    out_specs = P(("dp", "fsdp"), "seq", None, None)
    return jax.shard_map(shards, mesh=mesh, in_specs=in_specs, out_specs=out_specs, check_vma=False)
```

```python
import jax
import jax.numpy as jnp
from jax import lax
from jax.experimental import pallas as pl
from jax.experimental.pallas import tpu as pltpu
from jax.sharding import PartitionSpec as P

AXES = ("dp", "seq", "fsdp")
SHIFTS = (0, 1, 3, 2)
CHOOSE_COST = 9_000_000_000


def place(x, y, z, core):
    return ((z // 4) * 16 + x * 4 + y) * 8 + (z % 4) * 2 + core


def every_place():
    return [(x, y, z, c) for x in range(4) for y in range(4) for z in range(8) for c in range(2)]


def scatter_perm(shift):
    pairs = []
    for x in range(4):
        for y in range(4):
            j = (x + y) % 4
            origin = (x + 2) % 4 if shift == 2 else x
            for a in range(2):
                for c in range(2):
                    z = 2 * j + a
                    pairs.append((place(origin, y, z, c), place(x, y, (z + 2 * shift) % 8, c)))
    return pairs


def line_perm(shift):
    pairs = []
    for x, y, z, c in every_place():
        to = ((x + shift) % 4, y) if c == 0 else (x, (y + shift) % 4)
        pairs.append((place(x, y, z, c), place(to[0], to[1], z, c)))
    return pairs


def cross_perm(shift):
    pairs = []
    for x, y, z, c in every_place():
        to = (x, (y + shift) % 4) if c == 0 else ((x + shift) % 4, y)
        pairs.append((place(x, y, z, c), place(to[0], to[1], z, c)))
    return pairs


def ring_perm(step):
    return [(place(x, y, z, c), place(x, y, (z + step) % 8, c)) for x, y, z, c in every_place()]


def partner_perm(side):
    pairs = []
    for x, y, z, c in every_place():
        step = side * (1 - 2 * (x % 2))
        pairs.append((place(x, y, z, c), place((x + step) % 4, (y - step) % 4, z, c)))
    return pairs


def swap_perm():
    return [(place(x, y, z, c), place(x, y, z, 1 - c)) for x, y, z, c in every_place()]


def prepare_kernel(where, video, wq, wk, wv, f0, f1, f2, f3, q0, q1, q2, q3, frames, columns, packed, sems, out_sems):
    cross = jnp.where(where[2] == 0, where[4], where[3])
    step, height, quarter = frames.shape[2], columns.shape[1], packed.shape[2]
    fetch_columns = [pltpu.make_async_copy(w, columns.at[m], sems.at[m]) for m, w in enumerate((wq, wk, wv))]
    fetch_frames = []
    for s in range(4):
        at = pl.multiple_of((cross + s) % 4 * step, step)
        fetch_frames.append(
            pltpu.make_async_copy(video.at[0, :, pl.ds(at, step), :], frames.at[s], sems.at[3 + s])
        )
    for copy in fetch_columns + fetch_frames:
        copy.start()
    stores = []
    for copy in fetch_columns:
        copy.wait()
    for r, out in ((2, q2), (1, q1), (3, q3), (0, q0)):
        for m in range(3):
            at = pl.multiple_of((r + 2 * where[6]) % 4 * quarter, 128)
            packed[r, height * m : height * (m + 1), :] = columns[m, :, pl.ds(at, quarter)]
        stores.append(pltpu.make_async_copy(packed.at[r], out, out_sems.at[r]))
        stores[-1].start()
    for s, out in enumerate((f0, f1, f2, f3)):
        fetch_frames[s].wait()
        stores.append(pltpu.make_async_copy(frames.at[s], out, out_sems.at[4 + s]))
        stores[-1].start()
    for store in stores:
        store.wait()


def prepare(where, video, columns):
    _, frames, patches, d = video.shape
    height = columns[0].shape[0]
    anywhere = pl.BlockSpec(memory_space=pl.ANY)
    return pl.pallas_call(
        prepare_kernel,
        in_specs=[pl.BlockSpec(memory_space=pltpu.SMEM)] + [anywhere] * 4,
        out_specs=[anywhere] * 8,
        out_shape=[jax.ShapeDtypeStruct((frames, patches // 4, d), jnp.bfloat16)] * 4
        + [jax.ShapeDtypeStruct((3 * height, d // 4), jnp.bfloat16)] * 4,
        scratch_shapes=[
            pltpu.VMEM((4, frames, patches // 4, d), jnp.bfloat16),
            pltpu.VMEM((3, height, d), jnp.bfloat16),
            pltpu.VMEM((4, 3 * height, d // 4), jnp.bfloat16),
            pltpu.SemaphoreType.DMA((7,)),
            pltpu.SemaphoreType.DMA((8,)),
        ],
        compiler_params=pltpu.CompilerParams(vmem_limit_bytes=60 * 2**20),
        name="prepare",
    )(where, video, *columns)


def norm_kernel(f0, f1, f2, f3, gain, out):
    at = 0
    for ref in (f0, f1, f2, f3):
        for f in range(ref.shape[0]):
            values = ref[f].astype(jnp.float32)
            average = jnp.mean(values, axis=-1, keepdims=True)
            centred = values - average
            spread = jnp.mean(centred * centred, axis=-1, keepdims=True)
            normed = centred * lax.rsqrt(spread + 1e-06) * gain[...]
            out[at : at + ref.shape[1], :] = normed.astype(jnp.bfloat16)
            at += ref.shape[1]


def layer_normed(blocks, gain):
    vmem = pl.BlockSpec(memory_space=pltpu.VMEM)
    frames, patches, d = blocks[0].shape
    return pl.pallas_call(
        norm_kernel,
        in_specs=[vmem] * 5,
        out_specs=vmem,
        out_shape=jax.ShapeDtypeStruct((4 * frames * patches, d), jnp.bfloat16),
        compiler_params=pltpu.CompilerParams(vmem_limit_bytes=10 * 2**20),
        name="norm_rows",
    )(*blocks, gain.reshape(1, d))


def choose_kernel(where, q0, q1, q2, q3, out_ref, sem):
    quarter = (where[5] // 2 - where[1] + 4) % 4
    for r, ref in enumerate((q0, q1, q2, q3)):

        @pl.when(quarter == r)
        def _(ref=ref):
            copy = pltpu.make_async_copy(ref, out_ref, sem)
            copy.start()
            copy.wait()


def choose(where, parts):
    anywhere = pl.BlockSpec(memory_space=pl.ANY)
    return pl.pallas_call(
        choose_kernel,
        in_specs=[pl.BlockSpec(memory_space=pltpu.SMEM)] + [anywhere] * 4,
        out_specs=anywhere,
        out_shape=jax.ShapeDtypeStruct(parts[0].shape, parts[0].dtype),
        scratch_shapes=[pltpu.SemaphoreType.DMA],
        cost_estimate=pl.CostEstimate(flops=CHOOSE_COST, bytes_accessed=2**20, transcendentals=0),
        compiler_params=pltpu.CompilerParams(vmem_limit_bytes=4 * 2**20),
        name="choose_quarter",
    )(where, *parts)


NT = (((1,), (1,)), ((), ()))


def stack_kernel(r0, r1, r2, r3, out_ref):
    for i, ref in enumerate((r0, r1, r2, r3)):
        out_ref[256 * i : 256 * i + 256, :] = ref[...]


def stack(pieces):
    vmem = pl.BlockSpec(memory_space=pltpu.VMEM)
    rows, d = pieces[0].shape
    return pl.pallas_call(
        stack_kernel,
        in_specs=[vmem] * 4,
        out_specs=vmem,
        out_shape=jax.ShapeDtypeStruct((4 * rows, d), jnp.bfloat16),
        compiler_params=pltpu.CompilerParams(vmem_limit_bytes=16 * 2**20),
        name="stack_rows",
    )(*pieces)


def add_products(where, rows, weights, turn, offset, own, other, total, first):
    z = (where[0] + offset + 8) % 8
    r = (z // 2 - where[1] + 4) % 4
    quarter = weights.shape[-1]
    for core, ref in ((where[2], own), (1 - where[2], other)):
        for m in range(3):
            for g in range(3):
                to = pl.multiple_of((z % 2 * 128 + core * 96 + 32 * g) % 192, 32)
                low = 96 * m + 32 * g
                weights[turn, m, pl.ds(to, 32), :] = ref[low : low + 32, :]
    for m in range(3):
        weights[turn, m, 192:, :] = jnp.zeros((64, quarter), jnp.bfloat16)
    product = lax.dot_general(
        rows[:, pl.ds(pl.multiple_of(r * quarter, 128), quarter)],
        weights[turn].reshape(768, quarter),
        NT,
        preferred_element_type=jnp.float32,
    )
    product = product.reshape(total.shape[1:])
    if first:
        total[z % 2] = product
    else:
        total[z % 2] = total[z % 2] + product


def project_kernel(offsets, where, rows, *refs):
    pieces, total, weights = refs[: 2 * len(offsets)], refs[-2], refs[-1]
    for turn, offset in enumerate(offsets):
        own, other = pieces[2 * turn], pieces[2 * turn + 1]
        add_products(where, rows, weights, turn, offset, own, other, total, offset in (0, -1))


def project(where, rows, offsets, pieces, before=()):
    vmem = pl.BlockSpec(memory_space=pltpu.VMEM)
    quarter = rows.shape[1] // 4
    return pl.pallas_call(
        lambda *refs: project_kernel(offsets, *refs),
        in_specs=[pl.BlockSpec(memory_space=pltpu.SMEM)] + [vmem] * (1 + len(pieces) + len(before)),
        out_specs=vmem,
        out_shape=jax.ShapeDtypeStruct((2, 32, 4, 8, 768), jnp.float32),
        scratch_shapes=[pltpu.VMEM((len(offsets), 3, 256, quarter), jnp.bfloat16)],
        input_output_aliases={2 + len(pieces): 0} if before else {},
        compiler_params=pltpu.CompilerParams(vmem_limit_bytes=20 * 2**20),
        name="project",
    )(where, rows, *pieces, *before)


def head_columns(total, g, m, h):
    at = 256 * m
    if h == 1:
        halves = [total[half, :, g, :, at + 128 : at + 192] for half in range(2)]
        return jnp.concatenate(halves, axis=-1).reshape(256, 128)
    return total[h // 2, :, g, :, at : at + 128].reshape(256, 128)


def attend_kernel(where, rows, *refs):
    pieces, (qg_ref, kg_ref, before, out_ref, weights, total, found) = refs[:4], refs[4:]
    total[...] = before[...]
    for turn, offset in enumerate((-3, 3)):
        add_products(where, rows, weights, turn, offset, pieces[2 * turn], pieces[2 * turn + 1], total, False)

    @pl.when(where[0] >= 0)
    def _():
        gains = qg_ref[...] * kg_ref[...] * (128.0**-0.5)
        row_patch = lax.broadcasted_iota(jnp.int32, (256, 256), 0) % 8
        col_patch = lax.broadcasted_iota(jnp.int32, (256, 256), 1) % 8
        same = row_patch == col_patch
        for g in range(4):
            for h in range(3):
                q_rows = head_columns(total, g, 0, h).astype(jnp.bfloat16)
                k = head_columns(total, g, 1, h).astype(jnp.bfloat16).astype(jnp.float32)
                v = head_columns(total, g, 2, h).astype(jnp.bfloat16)
                q = q_rows.astype(jnp.float32)
                q_scale = lax.rsqrt(jnp.mean(q * q, axis=-1, keepdims=True) + 1e-06)
                k_scale = lax.rsqrt(jnp.mean(k * k, axis=-1, keepdims=True) + 1e-06)
                k_unit = (k * k_scale * gains).astype(jnp.bfloat16)
                scores = lax.dot_general(q_rows, k_unit, NT, preferred_element_type=jnp.float32)
                exps = jnp.where(same, jnp.exp(scores * q_scale), 0.0)
                probs = (exps / jnp.sum(exps, axis=-1, keepdims=True)).astype(jnp.bfloat16)
                out = jnp.dot(probs, v, preferred_element_type=jnp.float32)
                found[:, g, :, 128 * h : 128 * h + 128] = out.reshape(32, 8, 128)
        core = where[2]
        along = jnp.where(core == 0, where[3], where[4])
        cross = jnp.where(core == 0, where[4], where[3])
        for piece, shift in enumerate(SHIFTS):
            for s in range(4):
                line, side = (along - shift + 4) % 4, (cross - s + 4) % 4
                to = jnp.where(core == 0, 4 * line + side, 4 * side + line)
                frame = 8 * piece + 2 * s
                out_ref[to] = found[frame : frame + 2].reshape(64, 384).astype(jnp.bfloat16)


def attend(where, rows, pieces, query_gain, key_gain, before):
    vmem = pl.BlockSpec(memory_space=pltpu.VMEM)
    quarter = rows.shape[1] // 4
    return pl.pallas_call(
        attend_kernel,
        in_specs=[pl.BlockSpec(memory_space=pltpu.SMEM)] + [vmem] * (4 + len(pieces)),
        out_specs=vmem,
        scratch_shapes=[
            pltpu.VMEM((2, 3, 256, quarter), jnp.bfloat16),
            pltpu.VMEM((2, 32, 4, 8, 768), jnp.float32),
            pltpu.VMEM((32, 4, 8, 384), jnp.float32),
        ],
        out_shape=jax.ShapeDtypeStruct((16, 64, 384), jnp.bfloat16),
        compiler_params=pltpu.CompilerParams(vmem_limit_bytes=30 * 2**20),
        name="project_attend",
    )(where, rows, *pieces, query_gain.reshape(1, 128), key_gain.reshape(1, 128), before)


def assemble_kernel(where, recv_ref, out_ref):
    for core in range(2):

        @pl.when(where[2] == core)
        def _(core=core):
            for x in range(4):
                for y in range(4):
                    at, j = 32 * (y if core == 0 else x), (x + y) % 4
                    for f in range(2):
                        out_ref[0, f, at : at + 32, 384 * j : 384 * j + 384] = recv_ref[
                            4 * x + y, 32 * f : 32 * f + 32, :
                        ]


def assemble(received, where):
    return pl.pallas_call(
        assemble_kernel,
        in_specs=[pl.BlockSpec(memory_space=pltpu.SMEM), pl.BlockSpec(memory_space=pltpu.VMEM)],
        out_specs=pl.BlockSpec(memory_space=pltpu.VMEM),
        out_shape=jax.ShapeDtypeStruct((1, 2, 128, 1536), jnp.bfloat16),
        compiler_params=pltpu.CompilerParams(vmem_limit_bytes=40 * 2**20),
        name="assemble_heads",
    )(where, received)


def shards(video, norm_gain, w_query, w_key, w_value, query_gain, key_gain):
    seq = lax.axis_index("seq")
    fsdp = lax.axis_index("fsdp")
    z = lax.axis_index("dp") * 4 + fsdp // 2
    group = (seq // 4 + seq % 4) % 4
    turned = seq // 4 % 2
    where = jnp.stack([(z + 4 * turned) % 8, group, fsdp % 2, seq // 4, seq % 4, z, turned]).astype(jnp.int32)

    *blocks, q0, q1, q2, q3 = prepare(where, video, [w.T for w in (w_query, w_key, w_value)])
    with jax.named_scope("rows_cross"):
        blocks = [blocks[0]] + [lax.ppermute(blocks[s], AXES, cross_perm(s)) for s in (1, 2, 3)]
    with jax.named_scope("scatter"):
        q2, q1, q3 = [lax.ppermute(q, AXES, scatter_perm(r)) for r, q in ((2, q2), (1, q1), (3, q3))]
    part = choose(where, [q0, q1, q2, q3])

    home = layer_normed(blocks, norm_gain)
    with jax.named_scope("rows_line"):
        rows = stack([home] + [lax.ppermute(home, AXES, line_perm(s)) for s in SHIFTS[1:]])

    def swapped(piece):
        with jax.named_scope("swap"):
            return piece, lax.ppermute(piece, AXES, swap_perm())

    def onward(up, down):
        with jax.named_scope("ring"):
            return lax.ppermute(up, AXES, ring_perm(1)), lax.ppermute(down, AXES, ring_perm(-1))

    def partners(piece, side):
        with jax.named_scope("partner"):
            return lax.ppermute(piece, AXES, partner_perm(side))

    up1, down1 = onward(part, part)
    up2, down2 = onward(up1, down1)
    up2, down2, rows = lax.optimization_barrier((up2, down2, rows))
    up3, down3 = onward(up2, down2)
    half_turn = partners(part, 1)
    early = swapped(part) + swapped(up1) + swapped(down1) + swapped(up2) + swapped(down2)
    total = project(where, rows, (0, -1, 1, -2, 2), early)
    up3, down3, half_turn, total = lax.optimization_barrier((up3, down3, half_turn, total))
    total = project(where, rows, (4,), swapped(half_turn), (total,))
    late = swapped(up3) + swapped(down3)
    output = attend(where, rows, late, query_gain, key_gain, total)
    with jax.named_scope("heads_back"):
        received = lax.all_to_all(output, "seq", split_axis=0, concat_axis=0, tiled=True)
    return assemble(received, where)


def solution(mesh):
    in_specs = (
        P(("dp", "fsdp"), "seq", None, None),
        P(),
        P(None, ("dp", "fsdp")),
        P(None, ("dp", "fsdp")),
        P(None, ("dp", "fsdp")),
        P(),
        P(),
    )
    out_specs = P(("dp", "fsdp"), "seq", None, None)
    return jax.shard_map(shards, mesh=mesh, in_specs=in_specs, out_specs=out_specs, check_vma=False)
```
